32 devices in a mesh: site: 2 (over y), pt: 4 (over z), var: 2 (over x), cmp: 2 (over core).
Axes of the slice: x: 2, y: 2, z: 4, core: 2. Of those that a mesh axis runs over, the one named last changes fastest.
Arguments:
- strain_green: bfloat16 [5120, 24, 256], P(('site', 'pt'), None, 'cmp'), parts along dimension 0, may hold values from -2.390625 to 2.390625
- green_scale: float32 [40, 24], P(('site', 'pt')), parts along dimension 0, may hold values from 0.3 to 3
- mechanism: float32 [6, 2560], P(None, 'pt'), may hold values from -4 to 4
- slip_amplitude: bfloat16 [4, 32, 1536], P('pt', 'var'), may hold values from 0.19921875 to 2
- onset_time: float32 [4, 32, 1536], P('pt', 'var'), may hold values from 0 to 128
- rupture_row: int32 [4], replicated, may hold values from 0 to 3, each once
- rupture_blocks: int32 [4, 12], replicated, may hold values from 0 to 19, as said below
- block_count: int32 [4], replicated, may hold values from 1 to 12, 16 in all
- crossover: int32 [4], replicated, may hold values from 128 to 251
- high_band: float32 [8, 32, 2, 512], P(('site', 'pt'), 'var', None, 'cmp'), parts along dimension 0, may hold values from -6 to 6
Outputs:
- seismograms: float32 [8, 32, 2, 512], P(('site', 'pt'), 'var', None, 'cmp'), parts along dimension 0
The draws below stay inside these ranges and needn't reach their ends.
There are 2 independent parts, one for each index of `site`. The reference program is written for one: setup_inputs(seed, part) draws one part's arguments, and reference() takes and returns one part's arrays. A program takes and returns all parts, laid end to end along the dimension named above; an argument that names none is the same for every part. Nothing has to cross between parts.
Inputs may be any that keep to these rules, and one draw needn't show every extreme that they name: `rupture_blocks`: each row names 12 different point blocks; rupture r covers the first block_count[r] of them.
All inputs are finite; a program needn't handle non-finite values.
Results may differ from the reference program's by a relative error of at most 0.0028.
Values may be sent and summed in bfloat16 or wider, within the bound.
No kernel may reach another device: no remote copies, remote signals or barrier semaphores. Data moves between devices by JAX's collectives and lax.ppermute only.
A program may use at most 64 MiB of HBM per device.

```python
import math
import jax
import jax.numpy as jnp
import numpy as np
from jax import lax

BINS = 256
SAMPLES = 512
BLOCK = 128
MAXB = 12
NBLOCKS = 20
NPTS = 2560
RUPTURES = 4
VARS = 32


def draw_rupture_blocks(key, part):
    row_keys = jax.random.split(key, RUPTURES)
    shuffled = jax.vmap(lambda row_key: jax.random.permutation(row_key, NBLOCKS))(row_keys)
    return shuffled[:, :MAXB].astype(jnp.int32)


def plant(drawn, key, least, top_value):
    longest = drawn.shape.index(max(drawn.shape))
    spots = []
    for shift in (0, 1):
        where = [jax.random.randint(jax.random.fold_in(key, axis), (), 0, length) for axis, length in enumerate(drawn.shape)]
        where[longest] = (where[longest] + shift) % drawn.shape[longest]
        spots.append(tuple(where))
    return drawn.at[spots[0]].set(least).at[spots[1]].set(top_value)


def block_scale(rng, extent, shards, smallest, top_value):
    def one(dim, shards_of):
        draws = jax.random.uniform(jax.random.fold_in(jax.random.fold_in(rng, 6), dim), (shards_of,), jnp.float32, smallest / len(shards), top_value / len(shards))
        return jnp.repeat(jnp.exp(draws), extent[dim] // shards_of).reshape((-1,) + (1,) * (len(extent) - dim - 1))

    loudness = one(*shards[0])
    for cut in shards[1:]:
        loudness = loudness * one(*cut)
    return loudness


def profile(count, total, most, slope):
    portions = [(1 << 20) // math.isqrt(grade ** slope) + 1 for grade in range(2, count + 1)]
    rest, holding = total - most - (count - 1), [1] * (count - 1)
    while rest > 0:
        movable = [i for i in range(count - 1) if holding[i] < most]
        whole, remaining = sum([portions[i] for i in movable]), rest
        for i in movable:
            extra = min(most - holding[i], max(1, remaining * portions[i] // whole), rest)
            holding[i] = holding[i] + extra
            rest = rest - extra
    return np.array([most] + holding)


def uneven_parts(own_key, number_of, total, limit, lean):
    if number_of == 2:
        one = jax.random.randint(own_key, (), max(1, total - limit), min(limit, total - 1) + 1)
        return jnp.stack([one, total - one])
    sizes = jnp.asarray(profile(number_of, total, limit, lean), jnp.int32)
    couples = (number_of - 1) // 2
    source_of, receiver = sizes[1:1 + 2 * couples:2], sizes[2:2 + 2 * couples:2]
    slack = jnp.minimum(source_of - 1, limit - receiver)
    moved = jax.random.randint(jax.random.fold_in(own_key, 1), (couples,), 0, 1 << 20) % (slack + 1)
    sizes = sizes.at[1:1 + 2 * couples:2].set(source_of - moved).at[2:2 + 2 * couples:2].set(receiver + moved)
    return sizes[jax.random.permutation(jax.random.fold_in(own_key, 2), number_of)]


def centred(stream_key, extent, scale, limit, cuts=(), dtype=jnp.bfloat16):
    level = block_scale(stream_key, extent, cuts, -0.22, 0.18) if cuts else 1.0
    entries = jax.random.normal(stream_key, extent, jnp.float32) * scale * level
    return jnp.minimum(jnp.maximum(entries, -limit), limit).astype(dtype)


def setup_inputs(seed: int = 0, part: int = 0) -> dict:
    splits = jax.random.split(jax.random.key(seed), 11)
    part_splits = jax.random.split(jax.random.fold_in(splits[10], part), 11)
    return {
        "strain_green": centred(part_splits[0], (NPTS, 24, BINS), 0.3, 2.390625, ((0, 4), (2, 2))),
        "green_scale": jnp.clip(jnp.exp(math.log(3.0) - 2.3025851 * jax.random.uniform(part_splits[1], (NBLOCKS, 24), jnp.float32) ** block_scale(part_splits[1], (NBLOCKS, 24), ((0, 4),), -0.2, 0.2)), 0.3, 3.0),
        "mechanism": centred(splits[2], (6, NPTS), 1.0, 4.0, ((1, 4),), jnp.float32),
        "slip_amplitude": jnp.clip(jnp.exp(math.log(2.0) - 2.306499 * jax.random.uniform(splits[3], (RUPTURES, VARS, MAXB * BLOCK), jnp.float32) ** block_scale(splits[3], (RUPTURES, VARS, MAXB * BLOCK), ((0, 4), (1, 2)), -0.2, 0.2)), 0.19921875, 2.0).astype(jnp.bfloat16),
        "onset_time": jnp.clip(128.0 * jax.random.uniform(splits[4], (RUPTURES, VARS, MAXB * BLOCK), jnp.float32) ** block_scale(splits[4], (RUPTURES, VARS, MAXB * BLOCK), ((0, 4), (1, 2)), -0.2, 0.2), 0.0, 128.0),
        "rupture_row": jax.random.permutation(splits[5], RUPTURES).astype(jnp.int32),
        "rupture_blocks": draw_rupture_blocks(jax.random.fold_in(splits[10], 71), part),
        "block_count": uneven_parts(splits[7], RUPTURES, RUPTURES * (MAXB // 3), MAXB, 2).astype(jnp.int32),
        "crossover": plant(jax.random.randint(splits[8], (RUPTURES,), BINS // 2, BINS - 4), jax.random.fold_in(splits[8], 1), BINS // 2, (BINS - 4) - 1).astype(jnp.int32),
        "high_band": centred(part_splits[9], (RUPTURES, VARS, 2, SAMPLES), 1.0, 6.0, ((0, 4), (1, 2), (3, 2)), jnp.float32),
    }


taper_width = 8.0


def green_tensor(strain_green, green_scale, mechanism):
    points = strain_green.shape[0]
    bins_here = strain_green.shape[2]
    blocks_scale = jnp.repeat(green_scale, points // green_scale.shape[0], axis=0)
    factors = blocks_scale.reshape(points, 4, 6) * jnp.transpose(mechanism)[:, None, :]
    spectra = strain_green.reshape(points, 4, 6, bins_here).astype(jnp.float32)
    summed = jnp.einsum("pkjf,pkj->pkf", spectra, factors, precision=lax.Precision.HIGHEST)
    return summed.astype(jnp.bfloat16)


def block_term(green_block, amplitude, onset_block, phase_step):
    angles = onset_block[:, :, None] * phase_step[None, None, :]
    weight = amplitude.astype(jnp.float32)[:, :, None]
    with_cos = weight * jnp.cos(angles)
    with_sin = weight * jnp.sin(angles)
    green_wide = green_block.astype(jnp.float32)
    real_green = green_wide[:, 0:2]
    imag_green = green_wide[:, 2:4]
    highest = lax.Precision.HIGHEST
    real_part = jnp.einsum("vqf,qcf->vcf", with_cos, real_green, precision=highest) + jnp.einsum("vqf,qcf->vcf", with_sin, imag_green, precision=highest)
    imag_part = jnp.einsum("vqf,qcf->vcf", with_cos, imag_green, precision=highest) - jnp.einsum("vqf,qcf->vcf", with_sin, real_green, precision=highest)
    return jnp.concatenate([real_part, imag_part], axis=1)


def reference(strain_green, green_scale, mechanism, slip_amplitude, onset_time, rupture_row, rupture_blocks, block_count, crossover, high_band):
    highest = lax.Precision.HIGHEST
    green = green_tensor(strain_green, green_scale, mechanism)
    frequency = jnp.arange(BINS).astype(jnp.float32)
    phase_step = frequency * (2.0 * math.pi / SAMPLES)

    def one_row(position):
        rupture = rupture_row[position]
        blocks = rupture_blocks[rupture]
        covered = block_count[rupture]
        amplitudes = slip_amplitude[position]
        onsets = onset_time[position]

        def visit(running, slot_number):
            first_point = (blocks[slot_number] * BLOCK).astype(jnp.int32)
            green_block = lax.dynamic_slice_in_dim(green, first_point, BLOCK, 0)
            offset = (slot_number * BLOCK).astype(jnp.int32)
            amplitude = lax.dynamic_slice_in_dim(amplitudes, offset, BLOCK, 1)
            onset_block = lax.dynamic_slice_in_dim(onsets, offset, BLOCK, 1)
            contribution = block_term(green_block, amplitude, onset_block, phase_step)
            return running + jnp.where(slot_number < covered, contribution, jnp.zeros_like(contribution)), None

        running, unused = lax.scan(visit, jnp.zeros((VARS, 4, BINS), jnp.float32), jnp.arange(MAXB).astype(jnp.int32))
        return running

    spectrum = lax.map(one_row, jnp.arange(RUPTURES).astype(jnp.int32))
    samples_index = jnp.arange(SAMPLES).astype(jnp.int32)
    bins_index = jnp.arange(BINS).astype(jnp.int32)
    angles = ((bins_index[:, None] * samples_index[None, :]) % SAMPLES).astype(jnp.float32) * (2.0 * math.pi / SAMPLES)
    cosine = jnp.cos(angles)
    sine_table = jnp.sin(angles)
    band_rows = high_band.reshape(-1, SAMPLES)
    band_real = jnp.dot(band_rows, cosine.T, precision=highest)
    band_imag = -jnp.dot(band_rows, sine_table.T, precision=highest)
    crossing = crossover[rupture_row].astype(jnp.float32)
    taper_weight = jnp.clip((crossing[:, None] - frequency[None, :]) / taper_width + 0.5, 0.0, 1.0)
    taper_rows = jnp.repeat(taper_weight, VARS * 2, axis=0)
    spectrum_real = spectrum[:, :, 0:2].reshape(-1, BINS)
    spectrum_imag = spectrum[:, :, 2:4].reshape(-1, BINS)
    coefficient = jnp.where(bins_index == 0, 1.0, 2.0) / SAMPLES
    excess_real = taper_rows * (spectrum_real - band_real) * coefficient
    excess_imag = taper_rows * (spectrum_imag - band_imag) * coefficient
    basis_table = jnp.concatenate([cosine, -sine_table], axis=0)
    low_band = jnp.dot(jnp.concatenate([excess_real, excess_imag], axis=1), basis_table, precision=highest)
    return (band_rows + low_band).reshape(high_band.shape)
```

```python
import functools
import math

import jax
import jax.numpy as jnp
import ml_dtypes
import numpy as np
from jax import lax
from jax.experimental import pallas as pl
from jax.experimental.pallas import tpu as pltpu
from jax.sharding import PartitionSpec as P

taper_width = 8.0
f32 = jnp.float32
bf16 = jnp.bfloat16
highest = lax.Precision.HIGHEST
vmem_bytes = 48 * 1024 * 1024
SMEM = pl.BlockSpec(memory_space=pltpu.SMEM)
VMEM = pl.BlockSpec(memory_space=pltpu.VMEM)


def params():
    return pltpu.CompilerParams(vmem_limit_bytes=vmem_bytes)


def cost(flops, nbytes):
    return pl.CostEstimate(flops=flops, bytes_accessed=nbytes, transcendentals=0)


def split_table(table):
    high = table.astype(ml_dtypes.bfloat16)
    low = (table - high.astype(np.float64)).astype(ml_dtypes.bfloat16)
    return high, low


def fourier_table(bins, samples, samples_here):
    product = (np.arange(bins)[:, None] * np.arange(samples_here)[None, :]) % samples
    angle = product * (2.0 * np.pi / samples)
    return np.concatenate([np.cos(angle), -np.sin(angle)], axis=0)


def pack_kernel(blocks_here, block_points, row_ref, blocks_ref, count_ref, slip_ref, onset_ref, *outs):
    me = lax.axis_index("pt")
    rupture = row_ref[me]

    def visit(slot, carry):
        block = blocks_ref[rupture, slot]
        owner = block // blocks_here
        local = block - owner * blocks_here
        offset = pl.multiple_of(slot * block_points, block_points)
        onset = onset_ref[0, :, pl.ds(offset, block_points)]
        first = onset.astype(bf16)
        second = (onset - first.astype(f32)).astype(bf16)
        slip = slip_ref[0, :, pl.ds(offset, block_points)]
        for step, out in enumerate(outs):

            @pl.when(owner == jnp.bitwise_xor(me, step))
            def _():
                out[local, 0] = first
                out[local, 1] = second
                out[local, 2] = slip

        return carry

    lax.fori_loop(0, count_ref[rupture], visit, 0)


def green_kernel(strain_ref, scale_ref, mechanism_ref, out_ref):
    block_points, bins = mechanism_ref.shape[1], strain_ref.shape[1]
    rows = 24
    octet = 8
    wide = octet * rows
    column = lax.broadcasted_iota(jnp.int32, (6, wide), 1) % rows
    spread_six = (column % 6 == lax.broadcasted_iota(jnp.int32, (6, wide), 0)).astype(f32)
    column = lax.broadcasted_iota(jnp.int32, (rows, wide), 1) % rows
    spread_rows = (column == lax.broadcasted_iota(jnp.int32, (rows, wide), 0)).astype(f32)
    moments = lax.dot_general(
        mechanism_ref[...], spread_six, (((0,), (0,)), ((), ())), precision=highest,
        preferred_element_type=f32,
    )
    scales = jnp.dot(scale_ref[0], spread_rows, precision=highest, preferred_element_type=f32)
    factor = moments * scales
    column = lax.broadcasted_iota(jnp.int32, (octet, wide), 1)
    same_point = column // rows == lax.broadcasted_iota(jnp.int32, (octet, wide), 0)
    part = (column % rows) // 6
    masks = [same_point & (part == k) for k in range(4)]
    lane = lax.broadcasted_iota(jnp.int32, (2 * octet, bins), 1) % 4
    lanes = [lane == k for k in range(4)]
    low_lane = lane < 2
    for pair in range(block_points // (2 * octet)):
        spectra = [[], [], [], []]
        for half in range(2):
            first = pair * 2 * octet + half * octet
            here = factor[first : first + octet]
            coarse = here.astype(bf16).astype(f32)
            fine = here - coarse
            left = jnp.concatenate(
                [jnp.where(mask, coarse, 0.0) for mask in masks]
                + [jnp.where(mask, fine, 0.0) for mask in masks],
                axis=0,
            ).astype(bf16)
            strain = strain_ref[first * rows : first * rows + wide, :]
            both = jnp.dot(left, strain, preferred_element_type=f32)
            for k in range(4):
                spectra[k].append(
                    both[k * octet : (k + 1) * octet]
                    + both[(k + 4) * octet : (k + 5) * octet]
                )
        green = [jnp.concatenate(s, axis=0).astype(bf16).astype(f32) for s in spectra]
        place = pl.ds(pair * 2 * octet, 2 * octet)
        below = pl.ds(block_points + pair * 2 * octet, 2 * octet)
        for r in range(4):
            top = jnp.zeros_like(green[0])
            for k in range(4):
                moved = green[k] if k == r else pltpu.roll(green[k], (k - r) % bins, 1)
                top = jnp.where(lanes[k], moved, top)
            bottom = jnp.where(low_lane, pltpu.roll(top, bins - 2, 1), -pltpu.roll(top, 2, 1))
            out_ref[0, r, place, :] = top.astype(bf16)
            out_ref[0, r, below, :] = bottom.astype(bf16)


def circle(cycles):
    x = cycles - jnp.round(cycles)
    z = x * x * (math.pi * math.pi)
    sine, cosine = 0.0, 0.0
    for n in range(5, -1, -1):
        sine = sine * z + (-1.0) ** n / math.factorial(2 * n + 1)
    for n in range(6, -1, -1):
        cosine = cosine * z + (-1.0) ** n / math.factorial(2 * n)
    sine = sine * x * math.pi
    return 1.0 - 2.0 * sine * sine, 2.0 * sine * cosine


def turn(a, b):
    return a[0] * b[0] - a[1] * b[1], a[0] * b[1] + a[1] * b[0]


def spectra_kernel(blocks_here, samples, row_ref, blocks_ref, count_ref, green_ref, *refs):
    steps = (len(refs) - 2) // 2
    packed, outs, waves, total = refs[:steps], refs[steps : 2 * steps], refs[-2], refs[-1]
    variations, block_points = packed[0].shape[2:]
    bins = green_ref.shape[3]
    me = lax.axis_index("pt")
    lowest = me * blocks_here
    first_bin = (lax.axis_index("cmp") * bins).astype(f32)
    lane = lax.broadcasted_iota(jnp.int32, (variations, bins), 1)
    quarter = lane // 4
    for step in range(steps):
        source = packed[step]
        rupture = row_ref[jnp.bitwise_xor(me, step)]
        total[...] = jnp.zeros_like(total)

        def visit(slot, carry):
            local = blocks_ref[rupture, slot] - lowest

            @pl.when((local >= 0) & (local < blocks_here))
            def _():
                onset = source[local, 0].astype(f32) + source[local, 1].astype(f32)
                slip = source[local, 2].astype(f32)
                cycles = onset * (1.0 / samples)
                one = circle(cycles)
                two = turn(one, one)
                four = turn(two, two)
                start = circle(cycles * first_bin)
                now = [(slip * start[0], slip * start[1])]
                now.append(turn(now[0], one))
                now.append(turn(now[0], two))
                now.append(turn(now[1], two))
                after = [turn(wave, four) for wave in now]
                double = 2.0 * four[0]
                for j in range(bins // 4):
                    place = pl.ds(j * variations, variations)
                    for r in range(4):
                        waves[r, place, 0:block_points] = now[r][0].astype(bf16)
                        waves[r, place, block_points : 2 * block_points] = now[r][1].astype(bf16)
                    later = [
                        (double * after[r][0] - now[r][0], double * after[r][1] - now[r][1])
                        for r in range(4)
                    ]
                    now, after = after, later
                for r in range(4):
                    product = jnp.dot(waves[r], green_ref[local, r], preferred_element_type=f32)
                    found = product[0:variations]
                    for j in range(1, bins // 4):
                        found = jnp.where(
                            quarter == j, product[j * variations : (j + 1) * variations], found
                        )
                    total[r] += found

            return carry

        lax.fori_loop(0, count_ref[rupture], visit, 0)
        sums = [total[r] for r in range(4)]
        for k in range(4):
            spectrum = jnp.zeros_like(sums[0])
            for r in range(4):
                moved = sums[r] if k == r else pltpu.roll(sums[r], (r - k) % bins, 1)
                spectrum = jnp.where(lane % 4 == r, moved, spectrum)
            outs[step][k] = spectrum


def three_products(left, table_high, table_low):
    coarse = left.astype(bf16)
    fine = (left - coarse.astype(f32)).astype(bf16)
    return (
        jnp.dot(coarse, table_high, preferred_element_type=f32)
        + jnp.dot(fine, table_high, preferred_element_type=f32)
        + jnp.dot(coarse, table_low, preferred_element_type=f32)
    )


def half_sign(bins, columns):
    odd = lax.broadcasted_iota(jnp.int32, (1, columns), 1) % bins % 2
    return (1 - 2 * odd * lax.axis_index("cmp")).astype(f32)


def band_kernel(bins, high_ref, table_high, table_low, out_ref):
    rows = jnp.concatenate([high_ref[0, :, c, :] for c in range(2)], axis=0)
    band = three_products(rows, table_high[...], table_low[...])
    out_ref[...] = -band * half_sign(bins, 2 * bins)


def sum_kernel(bins_here, bins, band_ref, *refs):
    spectra, out_ref = refs[:-1], refs[-1]
    out_ref[...] = band_ref[...]
    half = lax.axis_index("cmp") * bins_here
    variations = spectra[0].shape[1]
    for k in range(4):
        piece = spectra[0][k]
        for other in spectra[1:]:
            piece = piece + other[k]
        place = pl.ds(pl.multiple_of((k // 2) * bins + half, bins_here), bins_here)
        rows = pl.ds((k % 2) * variations, variations)
        out_ref[rows, place] = out_ref[rows, place] + piece


def merge_kernel(
    bins, samples, row_ref, crossover_ref, own_ref, other_ref, high_ref, table_high, table_low, out_ref
):
    crossing = crossover_ref[row_ref[lax.axis_index("pt")]].astype(f32)
    column = lax.broadcasted_iota(jnp.int32, (1, 2 * bins), 1) % bins
    taper = jnp.clip((crossing - column.astype(f32)) / taper_width + 0.5, 0.0, 1.0)
    coefficient = jnp.where(column == 0, 1.0, 2.0) / samples
    weight = taper * coefficient * half_sign(bins, 2 * bins)
    excess = (own_ref[...] + other_ref[...]) * weight
    low = three_products(excess, table_high[...], table_low[...])
    variations = high_ref.shape[1]
    for c in range(2):
        out_ref[0, :, c, :] = high_ref[0, :, c, :] + low[c * variations : (c + 1) * variations]


def body(
    pt_size,
    strain_green,
    green_scale,
    mechanism,
    slip_amplitude,
    onset_time,
    rupture_row,
    rupture_blocks,
    block_count,
    crossover,
    high_band,
):
    points_here, strain_rows, bins_here = strain_green.shape
    blocks_here = green_scale.shape[0]
    block_points = points_here // blocks_here
    variations = slip_amplitude.shape[1]
    samples_here = high_band.shape[3]
    halves = 2
    bins = halves * bins_here
    samples = halves * samples_here
    assert slip_amplitude.shape[0] == 1 and pt_size & (pt_size - 1) == 0
    assert samples == 2 * bins and strain_rows == 24

    pack_shape = jax.ShapeDtypeStruct((blocks_here, 3, variations, block_points), bf16)
    packed = pl.pallas_call(
        functools.partial(pack_kernel, blocks_here, block_points),
        out_shape=[pack_shape] * pt_size,
        in_specs=[SMEM] * 3 + [VMEM] * 2,
        out_specs=[VMEM] * pt_size,
        compiler_params=params(),
        name="pack",
    )(rupture_row, rupture_blocks, block_count, slip_amplitude, onset_time)

    def swap(value, step):
        return lax.ppermute(value, "pt", [(i, i ^ step) for i in range(pt_size)])

    received = [packed[0]] + [swap(packed[step], step) for step in range(1, pt_size)]

    green = pl.pallas_call(
        green_kernel,
        grid=(blocks_here,),
        out_shape=jax.ShapeDtypeStruct((blocks_here, 4, 2 * block_points, bins_here), bf16),
        in_specs=[
            pl.BlockSpec((block_points * strain_rows, bins_here), lambda b: (b, 0)),
            pl.BlockSpec((1, 1, strain_rows), lambda b: (b, 0, 0)),
            pl.BlockSpec((6, block_points), lambda b: (0, b)),
        ],
        out_specs=pl.BlockSpec((1, 4, 2 * block_points, bins_here), lambda b: (b, 0, 0, 0)),
        compiler_params=params(),
        cost_estimate=cost(2 * points_here * strain_rows * bins_here, 6_000_000),
        name="green",
    )(
        strain_green.reshape(points_here * strain_rows, bins_here),
        green_scale.reshape(blocks_here, 1, strain_rows),
        mechanism,
    )

    spectrum_shape = jax.ShapeDtypeStruct((4, variations, bins_here), f32)
    spectra = pl.pallas_call(
        functools.partial(spectra_kernel, blocks_here, samples),
        out_shape=[spectrum_shape] * pt_size,
        in_specs=[SMEM] * 3 + [VMEM] * (1 + pt_size),
        out_specs=[VMEM] * pt_size,
        scratch_shapes=[
            pltpu.VMEM((4, variations * bins_here // 4, 2 * block_points), bf16),
            pltpu.VMEM((4, variations, bins_here), f32),
        ],
        compiler_params=params(),
        name="spectra",
    )(rupture_row, rupture_blocks, block_count, green, *received)

    gathered = [spectra[0]] + [swap(spectra[step], step) for step in range(1, pt_size)]

    table = fourier_table(bins, samples, samples_here)
    table_high, table_low = split_table(table)
    turned_high, turned_low = split_table(np.ascontiguousarray(table.T))
    rows = 2 * variations
    band = pl.pallas_call(
        functools.partial(band_kernel, bins),
        out_shape=jax.ShapeDtypeStruct((rows, 2 * bins), f32),
        in_specs=[VMEM] * 3,
        out_specs=VMEM,
        compiler_params=params(),
        cost_estimate=cost(6 * rows * samples_here * 2 * bins, 1_000_000),
        name="band",
    )(high_band, jnp.asarray(turned_high), jnp.asarray(turned_low))

    excess = pl.pallas_call(
        functools.partial(sum_kernel, bins_here, bins),
        out_shape=jax.ShapeDtypeStruct((rows, 2 * bins), f32),
        in_specs=[VMEM] * (1 + pt_size),
        out_specs=VMEM,
        compiler_params=params(),
        name="excess",
    )(band, *gathered)
    other = lax.ppermute(excess, "cmp", [(0, 1), (1, 0)])

    return pl.pallas_call(
        functools.partial(merge_kernel, bins, samples),
        out_shape=jax.ShapeDtypeStruct(high_band.shape, f32),
        in_specs=[SMEM] * 2 + [VMEM] * 5,
        out_specs=VMEM,
        compiler_params=params(),
        name="merge",
    )(rupture_row, crossover, excess, other, high_band, jnp.asarray(table_high), jnp.asarray(table_low))


def solution(mesh):
    assert mesh.shape["cmp"] == 2
    return jax.shard_map(
        functools.partial(body, mesh.shape["pt"]),
        mesh=mesh,
        in_specs=(
            P(("site", "pt"), None, "cmp"),
            P(("site", "pt"), None),
            P(None, "pt"),
            P("pt", "var", None),
            P("pt", "var", None),
            P(),
            P(),
            P(),
            P(),
            P(("site", "pt"), "var", None, "cmp"),
        ),
        out_specs=P(("site", "pt"), "var", None, "cmp"),
        check_vma=False,
    )
```

```python
import functools
import math

import jax
import jax.numpy as jnp
import ml_dtypes
import numpy as np
from jax import lax
from jax.experimental import pallas as pl
from jax.experimental.pallas import tpu as pltpu
from jax.sharding import PartitionSpec as P

taper_width = 8.0
f32 = jnp.float32
bf16 = jnp.bfloat16
highest = lax.Precision.HIGHEST
vmem_bytes = 32 * 1024 * 1024
SMEM = pl.BlockSpec(memory_space=pltpu.SMEM)
VMEM = pl.BlockSpec(memory_space=pltpu.VMEM)
HBM = pl.BlockSpec(memory_space=pltpu.HBM)


def in_hbm(*arrays):
    return [pltpu.with_memory_space_constraint(array, pltpu.HBM) for array in arrays]


def fetch(sources, targets, sems):
    copies = [
        pltpu.make_async_copy(source, target, sems.at[i])
        for i, (source, target) in enumerate(zip(sources, targets))
    ]
    for copy in copies:
        copy.start()
    return copies


def params():
    return pltpu.CompilerParams(vmem_limit_bytes=vmem_bytes)


def cost(flops, nbytes):
    return pl.CostEstimate(flops=flops, bytes_accessed=nbytes, transcendentals=0)


def split_table(table):
    high = table.astype(ml_dtypes.bfloat16)
    low = (table - high.astype(np.float64)).astype(ml_dtypes.bfloat16)
    return high, low


def fourier_table(bins, samples, samples_here):
    product = (np.arange(bins)[:, None] * np.arange(samples_here)[None, :]) % samples
    angle = product * (2.0 * np.pi / samples)
    return np.concatenate([np.cos(angle), -np.sin(angle)], axis=0)


def pack_kernel(blocks_here, block_points, *refs):
    sources, strain_hbm, outs, head_ref = refs[:5], refs[5], refs[6:-8], refs[-8]
    targets, sems, head_sem = refs[-7:-2], refs[-2], refs[-1]
    row_ref, blocks_ref, count_ref, slip_ref, onset_ref = targets
    copies = fetch(sources, targets, sems)
    head = pltpu.make_async_copy(strain_hbm.at[pl.ds(0, head_ref.shape[0])], head_ref, head_sem)
    head.start()
    for copy in copies:
        copy.wait()
    me = lax.axis_index("pt")
    rupture = row_ref[me]

    def visit(slot, carry):
        block = blocks_ref[rupture, slot]
        owner = block // blocks_here
        local = block - owner * blocks_here
        offset = pl.multiple_of(slot * block_points, block_points)
        onset = onset_ref[0, :, pl.ds(offset, block_points)]
        first = onset.astype(bf16)
        second = (onset - first.astype(f32)).astype(bf16)
        slip = slip_ref[0, :, pl.ds(offset, block_points)]
        for step, out in enumerate(outs):

            @pl.when(owner == jnp.bitwise_xor(me, step))
            def _():
                out[local, 0] = first
                out[local, 1] = second
                out[local, 2] = slip

        return carry

    lax.fori_loop(0, count_ref[rupture], visit, 0)
    head.wait()


def three_parts(values):
    parts = []
    for _ in range(3):
        parts.append(values.astype(bf16).astype(f32))
        values = values - parts[-1]
    return parts


def green_kernel(
    head_ref, strain_hbm, scale_hbm, mechanism_hbm, out_ref, strain_ref, factor_ref, scale_ref, mechanism_ref, sems, small_sems
):
    small = fetch((scale_hbm, mechanism_hbm), (scale_ref, mechanism_ref), small_sems)
    rows, octet = 24, 8
    wide = octet * rows
    blocks_here = scale_ref.shape[0]
    bins = strain_ref.shape[1]
    block_points = mechanism_ref.shape[1] // blocks_here
    per_block = block_points * rows

    def strain_copy(b, source=strain_hbm):
        place = pl.ds(pl.multiple_of(b * per_block, per_block), per_block)
        return pltpu.make_async_copy(source.at[place], strain_ref.at[place], sems.at[b])

    for b in range(blocks_here):
        strain_copy(b, head_ref if b * per_block < head_ref.shape[0] else strain_hbm).start()
    for copy in small:
        copy.wait()
    column = lax.broadcasted_iota(jnp.int32, (18, wide), 1) % rows
    spread_six = column % 6 == lax.broadcasted_iota(jnp.int32, (18, wide), 0) % 6
    column = lax.broadcasted_iota(jnp.int32, (3 * rows, wide), 1) % rows
    spread_rows = column == lax.broadcasted_iota(jnp.int32, (3 * rows, wide), 0) % rows
    moments = lax.dot_general(
        jnp.concatenate(three_parts(mechanism_ref[...]), axis=0).astype(bf16),
        spread_six.astype(f32).astype(bf16),
        (((0,), (0,)), ((), ())),
        preferred_element_type=f32,
    )
    scales = jnp.dot(
        jnp.concatenate(three_parts(scale_ref[...]), axis=1).astype(bf16),
        spread_rows.astype(f32).astype(bf16),
        preferred_element_type=f32,
    )
    for b in range(blocks_here):
        place = slice(b * block_points, (b + 1) * block_points)
        factor_ref[place, :] = moments[place] * scales[b : b + 1]
    row = lax.broadcasted_iota(jnp.int32, (2 * octet, wide), 0)
    column = lax.broadcasted_iota(jnp.int32, (2 * octet, wide), 1)
    same_point = column // rows == row % octet
    part = (column % rows) // 6
    masks = [
        jnp.where(same_point & (part == 2 * h + row // octet), 1.0, 0.0).astype(bf16)
        for h in range(2)
    ]
    lane = lax.broadcasted_iota(jnp.int32, (2 * octet, bins), 1) % 4
    lanes = [lane == k for k in range(4)]
    low_lane = lane < 2

    def one_block(b, carry):
        strain_copy(b).wait()
        for pair in range(block_points // (2 * octet)):
            spectra = [[], [], [], []]
            for half in range(2):
                first = pl.multiple_of(
                    b * block_points + pair * 2 * octet + half * octet, octet
                )
                here = factor_ref[pl.ds(first, octet)]
                here = jnp.concatenate([here, here], axis=0)
                coarse = here.astype(bf16)
                fine = (here - coarse.astype(f32)).astype(bf16)
                left = jnp.concatenate(
                    [coarse * masks[0], coarse * masks[1], fine * masks[0], fine * masks[1]],
                    axis=0,
                )
                strain = strain_ref[pl.ds(pl.multiple_of(first * rows, wide), wide), :]
                both = jnp.dot(left, strain, preferred_element_type=f32)
                for k in range(4):
                    spectra[k].append(
                        both[k * octet : (k + 1) * octet]
                        + both[(k + 4) * octet : (k + 5) * octet]
                    )
            green = [jnp.concatenate(s, axis=0).astype(bf16).astype(f32) for s in spectra]
            place = pl.ds(pair * 2 * octet, 2 * octet)
            below = pl.ds(block_points + pair * 2 * octet, 2 * octet)
            for r in range(4):
                top = green[0] if r == 0 else pltpu.roll(green[0], bins - r, 1)
                for k in range(1, 4):
                    moved = green[k] if k == r else pltpu.roll(green[k], (k - r) % bins, 1)
                    top = jnp.where(lanes[k], moved, top)
                bottom = jnp.where(low_lane, pltpu.roll(top, bins - 2, 1), -pltpu.roll(top, 2, 1))
                out_ref[b, r, place, :] = top.astype(bf16)
                out_ref[b, r, below, :] = bottom.astype(bf16)
        return carry

    lax.fori_loop(0, blocks_here, one_block, 0)


def circle(cycles):
    x = cycles - jnp.round(cycles)
    z = x * x * (math.pi * math.pi)
    sine, cosine = 0.0, 0.0
    for n in range(5, -1, -1):
        sine = sine * z + (-1.0) ** n / math.factorial(2 * n + 1)
    for n in range(6, -1, -1):
        cosine = cosine * z + (-1.0) ** n / math.factorial(2 * n)
    sine = sine * x * math.pi
    return 1.0 - 2.0 * sine * sine, 2.0 * sine * cosine


def turn(a, b):
    return a[0] * b[0] - a[1] * b[1], a[0] * b[1] + a[1] * b[0]


def spectra_kernel(blocks_here, samples, row_hbm, blocks_hbm, count_hbm, green_ref, *refs):
    steps = (len(refs) - 7) // 2
    packed, outs = refs[:steps][::-1], refs[steps : 2 * steps]
    waves, total, held, row_ref, blocks_ref, count_ref, sems = refs[-7:]
    scalars = fetch((row_hbm, blocks_hbm, count_hbm), (row_ref, blocks_ref, count_ref), sems)
    variations, block_points = packed[0].shape[2:]
    bins = green_ref.shape[3]
    me = lax.axis_index("pt")
    lowest = me * blocks_here
    first_bin = (lax.axis_index("cmp") * bins).astype(f32)
    lane = lax.broadcasted_iota(jnp.int32, (variations, bins), 1)
    quarter = lane // 4
    total[...] = jnp.zeros_like(total)
    for step in range(steps):
        held[step] = packed[step][...]
    for copy in scalars:
        copy.wait()

    def one_row(step, carry):
        rupture = row_ref[jnp.bitwise_xor(me, step)]

        def visit(slot, carry):
            local = blocks_ref[rupture, slot] - lowest

            @pl.when((local >= 0) & (local < blocks_here))
            def _():
                onset = held[step, local, 0].astype(f32) + held[step, local, 1].astype(f32)
                slip = held[step, local, 2].astype(f32)
                cycles = onset * (1.0 / samples)
                one = circle(cycles)
                two = turn(one, one)
                four = turn(two, two)
                start = circle(cycles * first_bin)
                now = [(slip * start[0], slip * start[1])]
                now.append(turn(now[0], one))
                now.append(turn(now[0], two))
                now.append(turn(now[1], two))
                after = [turn(wave, four) for wave in now]
                double = 2.0 * four[0]
                for j in range(bins // 4):
                    place = pl.ds(j * variations, variations)
                    for r in range(4):
                        waves[r, place, 0:block_points] = now[r][0].astype(bf16)
                        waves[r, place, block_points : 2 * block_points] = now[r][1].astype(bf16)
                    later = [
                        (double * after[r][0] - now[r][0], double * after[r][1] - now[r][1])
                        for r in range(4)
                    ]
                    now, after = after, later
                for r in range(4):
                    product = jnp.dot(waves[r], green_ref[local, r], preferred_element_type=f32)
                    found = product[0:variations]
                    for j in range(1, bins // 4):
                        found = jnp.where(
                            quarter == j, product[j * variations : (j + 1) * variations], found
                        )
                    total[step, r] += found

            return carry

        return lax.fori_loop(0, count_ref[rupture], visit, carry)

    lax.fori_loop(0, steps, one_row, 0)
    for step in range(steps):
        sums = [total[step, r] for r in range(4)]
        for k in range(4):
            spectrum = sums[0] if k == 0 else pltpu.roll(sums[0], bins - k, 1)
            for r in range(1, 4):
                moved = sums[r] if k == r else pltpu.roll(sums[r], (r - k) % bins, 1)
                spectrum = jnp.where(lane % 4 == r, moved, spectrum)
            outs[step][k] = spectrum


def scalar_scratch(arrays):
    return [pltpu.SMEM(array.shape, array.dtype) for array in arrays]


def spectra_call(rupture_row, rupture_blocks, block_count, green, received):
    pt_size = len(received)
    blocks_here, parts, variations, block_points = received[0].shape
    bins_here = green.shape[3]
    samples = 4 * bins_here
    scalars = (rupture_row, rupture_blocks, block_count)
    return pl.pallas_call(
        functools.partial(spectra_kernel, blocks_here, samples),
        out_shape=[jax.ShapeDtypeStruct((4, variations, bins_here), f32)] * pt_size,
        in_specs=[HBM] * 3 + [VMEM] * (1 + pt_size),
        out_specs=[VMEM] * pt_size,
        scratch_shapes=[
            pltpu.VMEM((4, variations * bins_here // 4, 2 * block_points), bf16),
            pltpu.VMEM((pt_size, 4, variations, bins_here), f32),
            pltpu.VMEM((pt_size, blocks_here, parts, variations, block_points), bf16),
        ]
        + scalar_scratch(scalars)
        + [pltpu.SemaphoreType.DMA((3,))],
        compiler_params=params(),
        name="spectra",
    )(*in_hbm(*scalars), green, *received[::-1])


def three_products(left, table_high, table_low):
    coarse = left.astype(bf16)
    fine = (left - coarse.astype(f32)).astype(bf16)
    return (
        jnp.dot(coarse, table_high, preferred_element_type=f32)
        + jnp.dot(fine, table_high, preferred_element_type=f32)
        + jnp.dot(coarse, table_low, preferred_element_type=f32)
    )


def half_sign(bins, columns):
    odd = lax.broadcasted_iota(jnp.int32, (1, columns), 1) % bins % 2
    return (1 - 2 * odd * lax.axis_index("cmp")).astype(f32)


def band_kernel(bins, high_ref, table_high, table_low, out_ref):
    rows = jnp.concatenate([high_ref[0, :, c, :] for c in range(2)], axis=0)
    band = three_products(rows, table_high[...], table_low[...])
    out_ref[...] = -band * half_sign(bins, 2 * bins)


def sum_kernel(bins_here, bins, band_ref, *refs):
    spectra, out_ref = refs[:-1], refs[-1]
    out_ref[...] = band_ref[...]
    half = lax.axis_index("cmp") * bins_here
    variations = spectra[0].shape[1]
    for k in range(4):
        piece = spectra[0][k]
        for other in spectra[1:]:
            piece = piece + other[k]
        place = pl.ds(pl.multiple_of((k // 2) * bins + half, bins_here), bins_here)
        rows = pl.ds((k % 2) * variations, variations)
        out_ref[rows, place] = out_ref[rows, place] + piece


def merge_kernel(
    bins, samples, row_ref, crossover_ref, own_ref, other_ref, high_ref, table_high, table_low, out_ref
):
    crossing = crossover_ref[row_ref[lax.axis_index("pt")]].astype(f32)
    column = lax.broadcasted_iota(jnp.int32, (1, 2 * bins), 1) % bins
    taper = jnp.clip((crossing - column.astype(f32)) / taper_width + 0.5, 0.0, 1.0)
    coefficient = jnp.where(column == 0, 1.0, 2.0) / samples
    weight = taper * coefficient * half_sign(bins, 2 * bins)
    excess = (own_ref[...] + other_ref[...]) * weight
    low = three_products(excess, table_high[...], table_low[...])
    variations = high_ref.shape[1]
    for c in range(2):
        out_ref[0, :, c, :] = high_ref[0, :, c, :] + low[c * variations : (c + 1) * variations]


def body(
    pt_size,
    strain_green,
    green_scale,
    mechanism,
    slip_amplitude,
    onset_time,
    rupture_row,
    rupture_blocks,
    block_count,
    crossover,
    high_band,
):
    points_here, strain_rows, bins_here = strain_green.shape
    blocks_here = green_scale.shape[0]
    block_points = points_here // blocks_here
    variations = slip_amplitude.shape[1]
    samples_here = high_band.shape[3]
    halves = 2
    bins = halves * bins_here
    samples = halves * samples_here
    assert slip_amplitude.shape[0] == 1 and pt_size & (pt_size - 1) == 0
    assert samples == 2 * bins and strain_rows == 24

    strain_lines = strain_green.reshape(points_here * strain_rows, bins_here)
    head_blocks = 1
    head_shape = jax.ShapeDtypeStruct((head_blocks * block_points * strain_rows, bins_here), bf16)
    pack_shape = jax.ShapeDtypeStruct((blocks_here, 3, variations, block_points), bf16)
    *packed, head = pl.pallas_call(
        functools.partial(pack_kernel, blocks_here, block_points),
        out_shape=[pack_shape] * pt_size + [head_shape],
        in_specs=[HBM] * 6,
        out_specs=[VMEM] * (pt_size + 1),
        scratch_shapes=scalar_scratch((rupture_row, rupture_blocks, block_count))
        + [pltpu.VMEM(a.shape, a.dtype) for a in (slip_amplitude, onset_time)]
        + [pltpu.SemaphoreType.DMA((5,)), pltpu.SemaphoreType.DMA],
        compiler_params=params(),
        name="pack",
    )(
        *in_hbm(
            rupture_row, rupture_blocks, block_count, slip_amplitude, onset_time, strain_lines
        )
    )

    def swap(value, step):
        return lax.ppermute(value, "pt", [(i, i ^ step) for i in range(pt_size)])

    def exchange(values):
        moved = [swap(values[step], step) for step in range(pt_size - 1, 0, -1)]
        return [values[0]] + moved[::-1]

    received = exchange(packed)

    green = pl.pallas_call(
        green_kernel,
        out_shape=jax.ShapeDtypeStruct((blocks_here, 4, 2 * block_points, bins_here), bf16),
        in_specs=[VMEM] + [HBM] * 3,
        out_specs=VMEM,
        scratch_shapes=[
            pltpu.VMEM(strain_lines.shape, bf16),
            pltpu.VMEM((points_here, 8 * strain_rows), f32),
            pltpu.VMEM(green_scale.shape, f32),
            pltpu.VMEM(mechanism.shape, f32),
            pltpu.SemaphoreType.DMA((blocks_here,)),
            pltpu.SemaphoreType.DMA((2,)),
        ],
        compiler_params=params(),
        cost_estimate=cost(2 * points_here * strain_rows * bins_here, 6_000_000),
        name="green",
    )(head, *in_hbm(strain_lines, green_scale, mechanism))

    spectra = spectra_call(rupture_row, rupture_blocks, block_count, green, received)
    gathered = exchange(spectra)

    table = fourier_table(bins, samples, samples_here)
    table_high, table_low = split_table(table)
    turned_high, turned_low = split_table(np.ascontiguousarray(table.T))
    rows = 2 * variations
    band = pl.pallas_call(
        functools.partial(band_kernel, bins),
        out_shape=jax.ShapeDtypeStruct((rows, 2 * bins), f32),
        in_specs=[VMEM] * 3,
        out_specs=VMEM,
        compiler_params=params(),
        cost_estimate=cost(6 * rows * samples_here * 2 * bins, 1_000_000),
        name="band",
    )(high_band, jnp.asarray(turned_high), jnp.asarray(turned_low))

    excess = pl.pallas_call(
        functools.partial(sum_kernel, bins_here, bins),
        out_shape=jax.ShapeDtypeStruct((rows, 2 * bins), f32),
        in_specs=[VMEM] * (1 + pt_size),
        out_specs=VMEM,
        compiler_params=params(),
        name="excess",
    )(band, *gathered[::-1])
    other = lax.ppermute(excess, "cmp", [(0, 1), (1, 0)])

    return pl.pallas_call(
        functools.partial(merge_kernel, bins, samples),
        out_shape=jax.ShapeDtypeStruct(high_band.shape, f32),
        in_specs=[SMEM] * 2 + [VMEM] * 5,
        out_specs=VMEM,
        compiler_params=params(),
        name="merge",
    )(rupture_row, crossover, excess, other, high_band, jnp.asarray(table_high), jnp.asarray(table_low))


def solution(mesh):
    assert mesh.shape["cmp"] == 2
    return jax.shard_map(
        functools.partial(body, mesh.shape["pt"]),
        mesh=mesh,
        in_specs=(
            P(("site", "pt"), None, "cmp"),
            P(("site", "pt"), None),
            P(None, "pt"),
            P("pt", "var", None),
            P("pt", "var", None),
            P(),
            P(),
            P(),
            P(),
            P(("site", "pt"), "var", None, "cmp"),
        ),
        out_specs=P(("site", "pt"), "var", None, "cmp"),
        check_vma=False,
    )
```

```python
import functools
import math

import jax
import jax.numpy as jnp
import ml_dtypes
import numpy as np
from jax import lax
from jax.experimental import pallas as pl
from jax.experimental.pallas import tpu as pltpu
from jax.sharding import PartitionSpec as P

taper_width = 8.0
f32 = jnp.float32
bf16 = jnp.bfloat16
highest = lax.Precision.HIGHEST
vmem_bytes = 32 * 1024 * 1024
SMEM = pl.BlockSpec(memory_space=pltpu.SMEM)
VMEM = pl.BlockSpec(memory_space=pltpu.VMEM)
HBM = pl.BlockSpec(memory_space=pltpu.HBM)


def in_hbm(*arrays):
    return [pltpu.with_memory_space_constraint(array, pltpu.HBM) for array in arrays]


def fetch(sources, targets, sems):
    copies = [
        pltpu.make_async_copy(source, target, sems.at[i])
        for i, (source, target) in enumerate(zip(sources, targets))
    ]
    for copy in copies:
        copy.start()
    return copies


def params():
    return pltpu.CompilerParams(vmem_limit_bytes=vmem_bytes)


def cost(flops, nbytes):
    return pl.CostEstimate(flops=flops, bytes_accessed=nbytes, transcendentals=0)


def split_table(table):
    high = table.astype(ml_dtypes.bfloat16)
    low = (table - high.astype(np.float64)).astype(ml_dtypes.bfloat16)
    return high, low


def fourier_table(bins, samples, samples_here):
    product = (np.arange(bins)[:, None] * np.arange(samples_here)[None, :]) % samples
    angle = product * (2.0 * np.pi / samples)
    return np.concatenate([np.cos(angle), -np.sin(angle)], axis=0)


def scalar_scratch(arrays):
    return [pltpu.SMEM(array.shape, array.dtype) for array in arrays]


def live_words(pt_size, blocks_here):
    steps_per_word = 30 // blocks_here
    return steps_per_word, pl.cdiv(pt_size, steps_per_word)


def pack_kernel(blocks_here, block_points, onset_scale, slip_scale, *refs):
    sources, strain_hbm, outs = refs[:5], refs[5], refs[6:-9]
    live_ref, head_ref, targets, sems, head_sem = refs[-9], refs[-8], refs[-7:-2], refs[-2], refs[-1]
    row_ref, blocks_ref, count_ref, slip_ref, onset_ref = targets
    copies = fetch(sources, targets, sems)
    head = pltpu.make_async_copy(strain_hbm.at[pl.ds(0, head_ref.shape[0])], head_ref, head_sem)
    head.start()
    for copy in copies[:3]:
        copy.wait()
    me = lax.axis_index("pt")
    rupture = row_ref[me]
    steps_per_word, words = live_words(len(outs), blocks_here)
    for word in range(words):

        def one_step(step, flags):
            other = row_ref[jnp.bitwise_xor(me, step)]

            def one_slot(slot, flags):
                local = blocks_ref[other, slot] - me * blocks_here
                bit = jnp.left_shift(1, local + (step - word * steps_per_word) * blocks_here)
                return jnp.where((local >= 0) & (local < blocks_here), flags | bit, flags)

            return lax.fori_loop(0, count_ref[other], one_slot, flags)

        last = min(len(outs), (word + 1) * steps_per_word)
        flags = lax.fori_loop(word * steps_per_word, last, one_step, 0)
        live_ref[word] = jnp.full(live_ref.shape[1:], flags, jnp.int32)
    for copy in copies[3:]:
        copy.wait()

    def visit(slot, carry):
        block = blocks_ref[rupture, slot]
        owner = block // blocks_here
        local = block - owner * blocks_here
        offset = pl.multiple_of(slot * block_points, block_points)
        onset = jnp.round(onset_ref[0, :, pl.ds(offset, block_points)] * onset_scale)
        onset = jnp.clip(onset.astype(jnp.int32) - 32768, -32768, 32767).astype(jnp.int16)
        slip = slip_ref[0, :, pl.ds(offset, block_points)].astype(f32) * slip_scale
        slip = slip.astype(jnp.int32).astype(jnp.int16)
        for step, out in enumerate(outs):

            @pl.when(owner == jnp.bitwise_xor(me, step))
            def _():
                out[local, 0] = onset
                out[local, 1] = slip

        return carry

    lax.fori_loop(0, count_ref[rupture], visit, 0)
    head.wait()


def three_parts(values):
    parts = []
    for _ in range(3):
        parts.append(values.astype(bf16).astype(f32))
        values = values - parts[-1]
    return parts


def green_kernel(
    head_ref, strain_hbm, scale_hbm, mechanism_hbm, out_ref, strain_ref, factor_ref, scale_ref, mechanism_ref, sems, small_sems
):
    small = fetch((scale_hbm, mechanism_hbm), (scale_ref, mechanism_ref), small_sems)
    rows, octet = 24, 8
    wide = octet * rows
    blocks_here = scale_ref.shape[0]
    bins = strain_ref.shape[1]
    block_points = mechanism_ref.shape[1] // blocks_here
    per_block = block_points * rows

    def strain_copy(b, source=strain_hbm):
        place = pl.ds(pl.multiple_of(b * per_block, per_block), per_block)
        return pltpu.make_async_copy(source.at[place], strain_ref.at[place], sems.at[b])

    for b in range(blocks_here):
        strain_copy(b, head_ref if b * per_block < head_ref.shape[0] else strain_hbm).start()
    for copy in small:
        copy.wait()
    column = lax.broadcasted_iota(jnp.int32, (18, wide), 1) % rows
    spread_six = column % 6 == lax.broadcasted_iota(jnp.int32, (18, wide), 0) % 6
    column = lax.broadcasted_iota(jnp.int32, (3 * rows, wide), 1) % rows
    spread_rows = column == lax.broadcasted_iota(jnp.int32, (3 * rows, wide), 0) % rows
    moments = lax.dot_general(
        jnp.concatenate(three_parts(mechanism_ref[...]), axis=0).astype(bf16),
        spread_six.astype(f32).astype(bf16),
        (((0,), (0,)), ((), ())),
        preferred_element_type=f32,
    )
    scales = jnp.dot(
        jnp.concatenate(three_parts(scale_ref[...]), axis=1).astype(bf16),
        spread_rows.astype(f32).astype(bf16),
        preferred_element_type=f32,
    )
    for b in range(blocks_here):
        place = slice(b * block_points, (b + 1) * block_points)
        factor_ref[place, :] = moments[place] * scales[b : b + 1]
    row = lax.broadcasted_iota(jnp.int32, (2 * octet, wide), 0)
    column = lax.broadcasted_iota(jnp.int32, (2 * octet, wide), 1)
    same_point = column // rows == row % octet
    part = (column % rows) // 6
    masks = [
        jnp.where(same_point & (part == 2 * h + row // octet), 1.0, 0.0).astype(bf16)
        for h in range(2)
    ]
    lane = lax.broadcasted_iota(jnp.int32, (2 * octet, bins), 1) % 4
    lanes = [lane == k for k in range(4)]
    low_lane = lane < 2

    def one_block(b, carry):
        strain_copy(b).wait()
        for pair in range(block_points // (2 * octet)):
            spectra = [[], [], [], []]
            for half in range(2):
                first = pl.multiple_of(
                    b * block_points + pair * 2 * octet + half * octet, octet
                )
                here = factor_ref[pl.ds(first, octet)]
                here = jnp.concatenate([here, here], axis=0)
                coarse = here.astype(bf16)
                fine = (here - coarse.astype(f32)).astype(bf16)
                left = jnp.concatenate(
                    [coarse * masks[0], coarse * masks[1], fine * masks[0], fine * masks[1]],
                    axis=0,
                )
                strain = strain_ref[pl.ds(pl.multiple_of(first * rows, wide), wide), :]
                both = jnp.dot(left, strain, preferred_element_type=f32)
                for k in range(4):
                    spectra[k].append(
                        both[k * octet : (k + 1) * octet]
                        + both[(k + 4) * octet : (k + 5) * octet]
                    )
            green = [jnp.concatenate(s, axis=0).astype(bf16).astype(f32) for s in spectra]
            place = pl.ds(pair * 2 * octet, 2 * octet)
            below = pl.ds(block_points + pair * 2 * octet, 2 * octet)
            for r in range(4):
                top = green[0] if r == 0 else pltpu.roll(green[0], bins - r, 1)
                for k in range(1, 4):
                    moved = green[k] if k == r else pltpu.roll(green[k], (k - r) % bins, 1)
                    top = jnp.where(lanes[k], moved, top)
                bottom = jnp.where(low_lane, pltpu.roll(top, bins - 2, 1), -pltpu.roll(top, 2, 1))
                out_ref[b, r, place, :] = top.astype(bf16)
                out_ref[b, r, below, :] = bottom.astype(bf16)
        return carry

    lax.fori_loop(0, blocks_here, one_block, 0)


def circle(cycles):
    x = cycles - jnp.round(cycles)
    z = x * x * (math.pi * math.pi)
    sine, cosine = 0.0, 0.0
    for n in range(5, -1, -1):
        sine = sine * z + (-1.0) ** n / math.factorial(2 * n + 1)
    for n in range(6, -1, -1):
        cosine = cosine * z + (-1.0) ** n / math.factorial(2 * n)
    sine = sine * x * math.pi
    return 1.0 - 2.0 * sine * sine, 2.0 * sine * cosine


def turn(a, b):
    return a[0] * b[0] - a[1] * b[1], a[0] * b[1] + a[1] * b[0]


def spectra_kernel(blocks_here, samples, first_step, onset_scale, slip_scale, live_ref, green_ref, *refs):
    steps = (len(refs) - 3) // 2
    packed, outs = refs[:steps][::-1], refs[steps : 2 * steps]
    waves, total, held = refs[-3:]
    variations, block_points = packed[0].shape[2:]
    bins = green_ref.shape[3]
    first_bin = (lax.axis_index("cmp") * bins).astype(f32)
    quarter = lax.broadcasted_iota(jnp.int32, (variations, bins), 1) // 4
    total[...] = jnp.zeros_like(total)
    for step in range(steps):
        held[step * blocks_here : (step + 1) * blocks_here] = packed[step][...]
    steps_per_word, words = live_words(first_step + steps, blocks_here)
    for word in range(words):
        flags = jnp.max(live_ref[word])
        low = max(first_step, word * steps_per_word)
        high = min(first_step + steps, (word + 1) * steps_per_word)

        def visit(place, carry):
            flag = jnp.right_shift(flags, place - word * steps_per_word * blocks_here) & 1

            @pl.when(flag == 1)
            def _():
                step = place // blocks_here
                local = place - step * blocks_here
                source = place - first_step * blocks_here
                onset = held[source, 0].astype(jnp.int32).astype(f32) + 32768.0
                slip = held[source, 1].astype(jnp.int32).astype(f32) * (1.0 / slip_scale)
                cycles = onset * (1.0 / (onset_scale * samples))
                one = circle(cycles)
                two = turn(one, one)
                four = turn(two, two)
                start = circle(cycles * first_bin)
                now = [(slip * start[0], slip * start[1])]
                now.append(turn(now[0], one))
                now.append(turn(now[0], two))
                now.append(turn(now[1], two))
                after = [turn(wave, four) for wave in now]
                double = 2.0 * four[0]
                for j in range(bins // 4):
                    rows = pl.ds(j * variations, variations)
                    for r in range(4):
                        waves[r, rows, 0:block_points] = now[r][0].astype(bf16)
                        waves[r, rows, block_points : 2 * block_points] = now[r][1].astype(bf16)
                    later = [
                        (double * after[r][0] - now[r][0], double * after[r][1] - now[r][1])
                        for r in range(4)
                    ]
                    now, after = after, later
                for r in range(4):
                    product = jnp.dot(waves[r], green_ref[local, r], preferred_element_type=f32)
                    found = product[0:variations]
                    for j in range(1, bins // 4):
                        found = jnp.where(
                            quarter == j, product[j * variations : (j + 1) * variations], found
                        )
                    total[step - first_step, r] += found

            return carry

        lax.fori_loop(low * blocks_here, high * blocks_here, visit, 0)
    for step in range(steps):
        outs[step][...] = total[step]


def spectra_call(first_step, onset_scale, slip_scale, live, green, received, name):
    steps = len(received)
    blocks_here, parts, variations, block_points = received[0].shape
    bins_here = green.shape[3]
    return pl.pallas_call(
        functools.partial(
            spectra_kernel, blocks_here, 4 * bins_here, first_step, onset_scale, slip_scale
        ),
        out_shape=[jax.ShapeDtypeStruct((4, variations, bins_here), f32)] * steps,
        in_specs=[VMEM] * (2 + steps),
        out_specs=[VMEM] * steps,
        scratch_shapes=[
            pltpu.VMEM((4, variations * bins_here // 4, 2 * block_points), bf16),
            pltpu.VMEM((steps, 4, variations, bins_here), f32),
            pltpu.VMEM((steps * blocks_here, parts, variations, block_points), jnp.int16),
        ],
        compiler_params=params(),
        cost_estimate=cost(steps * 1_000_000_000, 4_000_000 * steps),
        name=name,
    )(live, green, *received[::-1])


def three_products(left, table_high, table_low):
    rows = left.shape[0]
    coarse = left.astype(bf16)
    fine = (left - coarse.astype(f32)).astype(bf16)
    both = jnp.dot(
        jnp.concatenate([coarse, fine], axis=0), table_high, preferred_element_type=f32
    )
    return both[:rows] + both[rows:] + jnp.dot(coarse, table_low, preferred_element_type=f32)


def half_sign(bins, columns):
    odd = lax.broadcasted_iota(jnp.int32, (1, columns), 1) % bins % 2
    return (1 - 2 * odd * lax.axis_index("cmp")).astype(f32)


def band_kernel(
    bins, samples, row_ref, crossover_ref, high_ref, table_high, table_low, out_ref, weight_ref
):
    rows = jnp.concatenate([high_ref[0, :, c, :] for c in range(2)], axis=0)
    band = three_products(rows, table_high[...], table_low[...])
    sign = half_sign(bins, 2 * bins)
    out_ref[...] = -band * sign
    crossing = crossover_ref[row_ref[lax.axis_index("pt")]].astype(f32)
    column = lax.broadcasted_iota(jnp.int32, weight_ref.shape, 1) % bins
    taper = jnp.clip((crossing - column.astype(f32)) / taper_width + 0.5, 0.0, 1.0)
    weight_ref[...] = taper * (jnp.where(column == 0, 1.0, 2.0) / samples) * sign


def sum_kernel(bins_here, bins, band_ref, *refs):
    spectra, out_ref = refs[:-1], refs[-1]
    out_ref[...] = band_ref[...]
    half = lax.axis_index("cmp") * bins_here
    variations = spectra[0].shape[1]
    sums = []
    for r in range(4):
        piece = spectra[0][r]
        for other in spectra[1:]:
            piece = piece + other[r]
        sums.append(piece)
    lane = lax.broadcasted_iota(jnp.int32, (variations, bins_here), 1) % 4
    for k in range(4):
        spectrum = sums[0] if k == 0 else pltpu.roll(sums[0], bins_here - k, 1)
        for r in range(1, 4):
            moved = sums[r] if k == r else pltpu.roll(sums[r], (r - k) % bins_here, 1)
            spectrum = jnp.where(lane == r, moved, spectrum)
        place = pl.ds(pl.multiple_of((k // 2) * bins + half, bins_here), bins_here)
        rows = pl.ds((k % 2) * variations, variations)
        out_ref[rows, place] = out_ref[rows, place] + spectrum


def merge_kernel(own_ref, other_ref, weight_ref, high_ref, table_high, table_low, out_ref):
    excess = (own_ref[...] + other_ref[...]) * weight_ref[0:1]
    low = three_products(excess, table_high[...], table_low[...])
    variations = high_ref.shape[1]
    for c in range(2):
        out_ref[0, :, c, :] = high_ref[0, :, c, :] + low[c * variations : (c + 1) * variations]


def body(
    pt_size,
    strain_green,
    green_scale,
    mechanism,
    slip_amplitude,
    onset_time,
    rupture_row,
    rupture_blocks,
    block_count,
    crossover,
    high_band,
):
    points_here, strain_rows, bins_here = strain_green.shape
    blocks_here = green_scale.shape[0]
    block_points = points_here // blocks_here
    variations = slip_amplitude.shape[1]
    samples_here = high_band.shape[3]
    halves = 2
    bins = halves * bins_here
    samples = halves * samples_here
    assert slip_amplitude.shape[0] == 1 and pt_size & (pt_size - 1) == 0
    assert samples == 2 * bins and strain_rows == 24

    strain_lines = strain_green.reshape(points_here * strain_rows, bins_here)
    head_blocks = 1
    head_shape = jax.ShapeDtypeStruct((head_blocks * block_points * strain_rows, bins_here), bf16)
    pack_shape = jax.ShapeDtypeStruct((blocks_here, 2, variations, block_points), jnp.int16)
    live_shape = jax.ShapeDtypeStruct((live_words(pt_size, blocks_here)[1], 8, 128), jnp.int32)
    onset_scale, slip_scale = 512.0, 1024.0
    *packed, live, head = pl.pallas_call(
        functools.partial(pack_kernel, blocks_here, block_points, onset_scale, slip_scale),
        out_shape=[pack_shape] * pt_size + [live_shape, head_shape],
        in_specs=[HBM] * 6,
        out_specs=[VMEM] * (pt_size + 2),
        scratch_shapes=scalar_scratch((rupture_row, rupture_blocks, block_count))
        + [pltpu.VMEM(a.shape, a.dtype) for a in (slip_amplitude, onset_time)]
        + [pltpu.SemaphoreType.DMA((5,)), pltpu.SemaphoreType.DMA],
        compiler_params=params(),
        name="pack",
    )(
        *in_hbm(
            rupture_row, rupture_blocks, block_count, slip_amplitude, onset_time, strain_lines
        )
    )

    def swap(value, step):
        return lax.ppermute(value, "pt", [(i, i ^ step) for i in range(pt_size)])

    def exchange(values):
        moved = [swap(values[step], step) for step in range(pt_size - 1, 0, -1)]
        return [values[0]] + moved[::-1]

    received = exchange(packed)

    green = pl.pallas_call(
        green_kernel,
        out_shape=jax.ShapeDtypeStruct((blocks_here, 4, 2 * block_points, bins_here), bf16),
        in_specs=[VMEM] + [HBM] * 3,
        out_specs=VMEM,
        scratch_shapes=[
            pltpu.VMEM(strain_lines.shape, bf16),
            pltpu.VMEM((points_here, 8 * strain_rows), f32),
            pltpu.VMEM(green_scale.shape, f32),
            pltpu.VMEM(mechanism.shape, f32),
            pltpu.SemaphoreType.DMA((blocks_here,)),
            pltpu.SemaphoreType.DMA((2,)),
        ],
        compiler_params=params(),
        cost_estimate=cost(2 * points_here * strain_rows * bins_here, 6_000_000),
        name="green",
    )(head, *in_hbm(strain_lines, green_scale, mechanism))

    sent = spectra_call(1, onset_scale, slip_scale, live, green, received[1:], "spectra")
    gathered = exchange([None] + list(sent))
    gathered[0], = spectra_call(0, onset_scale, slip_scale, live, green, received[:1], "own")

    table = fourier_table(bins, samples, samples_here)
    table_high, table_low = split_table(table)
    turned_high, turned_low = split_table(np.ascontiguousarray(table.T))
    rows = 2 * variations
    band, weight = pl.pallas_call(
        functools.partial(band_kernel, bins, samples),
        out_shape=[
            jax.ShapeDtypeStruct((rows, 2 * bins), f32),
            jax.ShapeDtypeStruct((8, 2 * bins), f32),
        ],
        in_specs=[SMEM] * 2 + [VMEM] * 3,
        out_specs=[VMEM] * 2,
        compiler_params=params(),
        cost_estimate=cost(6 * rows * samples_here * 2 * bins, 1_000_000),
        name="band",
    )(rupture_row, crossover, high_band, jnp.asarray(turned_high), jnp.asarray(turned_low))

    excess = pl.pallas_call(
        functools.partial(sum_kernel, bins_here, bins),
        out_shape=jax.ShapeDtypeStruct((rows, 2 * bins), f32),
        in_specs=[VMEM] * (1 + pt_size),
        out_specs=VMEM,
        compiler_params=params(),
        name="excess",
    )(band, *gathered[::-1])
    other = lax.ppermute(excess, "cmp", [(0, 1), (1, 0)])

    return pl.pallas_call(
        merge_kernel,
        out_shape=jax.ShapeDtypeStruct(high_band.shape, f32),
        in_specs=[VMEM] * 6,
        out_specs=VMEM,
        compiler_params=params(),
        name="merge",
    )(excess, other, weight, high_band, jnp.asarray(table_high), jnp.asarray(table_low))


def solution(mesh):
    assert mesh.shape["cmp"] == 2
    return jax.shard_map(
        functools.partial(body, mesh.shape["pt"]),
        mesh=mesh,
        in_specs=(
            P(("site", "pt"), None, "cmp"),
            P(("site", "pt"), None),
            P(None, "pt"),
            P("pt", "var", None),
            P("pt", "var", None),
            P(),
            P(),
            P(),
            P(),
            P(("site", "pt"), "var", None, "cmp"),
        ),
        out_specs=P(("site", "pt"), "var", None, "cmp"),
        check_vma=False,
    )
```

```python
import functools
import math

import jax
import jax.numpy as jnp
import ml_dtypes
import numpy as np
from jax import lax
from jax.experimental import pallas as pl
from jax.experimental.pallas import tpu as pltpu
from jax.sharding import PartitionSpec as P

taper_width = 8.0
f32 = jnp.float32
bf16 = jnp.bfloat16
highest = lax.Precision.HIGHEST
vmem_bytes = 32 * 1024 * 1024
SMEM = pl.BlockSpec(memory_space=pltpu.SMEM)
VMEM = pl.BlockSpec(memory_space=pltpu.VMEM)
HBM = pl.BlockSpec(memory_space=pltpu.HBM)


def in_hbm(*arrays):
    return [pltpu.with_memory_space_constraint(array, pltpu.HBM) for array in arrays]


def fetch(sources, targets, sems):
    copies = [
        pltpu.make_async_copy(source, target, sems.at[i])
        for i, (source, target) in enumerate(zip(sources, targets))
    ]
    for copy in copies:
        copy.start()
    return copies


def params():
    return pltpu.CompilerParams(vmem_limit_bytes=vmem_bytes)


def cost(flops, nbytes):
    return pl.CostEstimate(flops=flops, bytes_accessed=nbytes, transcendentals=0)


def split_table(table):
    high = table.astype(ml_dtypes.bfloat16)
    low = (table - high.astype(np.float64)).astype(ml_dtypes.bfloat16)
    return high, low


def fourier_table(bins, samples, samples_here):
    product = (np.arange(bins)[:, None] * np.arange(samples_here)[None, :]) % samples
    angle = product * (2.0 * np.pi / samples)
    return np.concatenate([np.cos(angle), -np.sin(angle)], axis=0)


def scalar_scratch(arrays):
    return [pltpu.SMEM(array.shape, array.dtype) for array in arrays]


def live_words(pt_size, blocks_here):
    steps_per_word = 30 // blocks_here
    return steps_per_word, pl.cdiv(pt_size, steps_per_word)


def pack_kernel(blocks_here, block_points, onset_scale, slip_scale, *refs):
    sources, strain_hbm, outs = refs[:5], refs[5], refs[6:-9]
    live_ref, head_ref, targets, sems, head_sem = refs[-9], refs[-8], refs[-7:-2], refs[-2], refs[-1]
    row_ref, blocks_ref, count_ref, slip_ref, onset_ref = targets
    copies = fetch(sources, targets, sems)
    head = pltpu.make_async_copy(strain_hbm.at[pl.ds(0, head_ref.shape[0])], head_ref, head_sem)
    head.start()
    for copy in copies[:3]:
        copy.wait()
    me = lax.axis_index("pt")
    rupture = row_ref[me]
    steps_per_word, words = live_words(len(outs), blocks_here)
    for word in range(words):

        def one_step(step, flags):
            other = row_ref[jnp.bitwise_xor(me, step)]

            def one_slot(slot, flags):
                local = blocks_ref[other, slot] - me * blocks_here
                bit = jnp.left_shift(1, local + (step - word * steps_per_word) * blocks_here)
                return jnp.where((local >= 0) & (local < blocks_here), flags | bit, flags)

            return lax.fori_loop(0, count_ref[other], one_slot, flags)

        last = min(len(outs), (word + 1) * steps_per_word)
        flags = lax.fori_loop(word * steps_per_word, last, one_step, 0)
        live_ref[word] = jnp.full(live_ref.shape[1:], flags, jnp.int32)
    for copy in copies[3:]:
        copy.wait()

    def visit(slot, carry):
        block = blocks_ref[rupture, slot]
        owner = block // blocks_here
        local = block - owner * blocks_here
        offset = pl.multiple_of(slot * block_points, block_points)
        onset = jnp.round(onset_ref[0, :, pl.ds(offset, block_points)] * onset_scale)
        onset = jnp.clip(onset.astype(jnp.int32) - 32768, -32768, 32767).astype(jnp.int16)
        slip = slip_ref[0, :, pl.ds(offset, block_points)].astype(f32) * slip_scale
        slip = slip.astype(jnp.int32).astype(jnp.int16)
        for step, out in enumerate(outs):

            @pl.when(owner == jnp.bitwise_xor(me, step))
            def _():
                out[local, 0] = onset
                out[local, 1] = slip

        return carry

    lax.fori_loop(0, count_ref[rupture], visit, 0)
    head.wait()


def three_parts(values):
    parts = []
    for _ in range(3):
        parts.append(values.astype(bf16).astype(f32))
        values = values - parts[-1]
    return parts


def green_kernel(
    steps, live_ref, head_ref, strain_hbm, scale_hbm, mechanism_hbm, out_ref, strain_ref, factor_ref, scale_ref, mechanism_ref, sems, small_sems
):
    small = fetch((scale_hbm, mechanism_hbm), (scale_ref, mechanism_ref), small_sems)
    rows, octet = 24, 8
    wide, depth = octet * rows, factor_ref.shape[1]
    blocks_here = scale_ref.shape[0]
    bins = strain_ref.shape[2]
    block_points = mechanism_ref.shape[1] // blocks_here
    per_block = block_points * rows

    def strain_copy(b, source=strain_hbm):
        place = pl.ds(pl.multiple_of(b * per_block, per_block), per_block)
        target = strain_ref.at[b, pl.ds(0, per_block)]
        return pltpu.make_async_copy(source.at[place], target, sems.at[b])

    for b in range(blocks_here):
        strain_copy(b, head_ref if b * per_block < head_ref.shape[0] else strain_hbm).start()
    for b in range(blocks_here):
        strain_ref[b, per_block:, :] = jnp.zeros((depth - wide, bins), bf16)
    for copy in small:
        copy.wait()
    column = lax.broadcasted_iota(jnp.int32, (18, depth), 1) % rows
    spread_six = column % 6 == lax.broadcasted_iota(jnp.int32, (18, depth), 0) % 6
    column = lax.broadcasted_iota(jnp.int32, (3 * rows, depth), 1) % rows
    spread_rows = column == lax.broadcasted_iota(jnp.int32, (3 * rows, depth), 0) % rows
    moments = lax.dot_general(
        jnp.concatenate(three_parts(mechanism_ref[...]), axis=0).astype(bf16),
        spread_six.astype(f32).astype(bf16),
        (((0,), (0,)), ((), ())),
        preferred_element_type=f32,
    )
    scales = jnp.dot(
        jnp.concatenate(three_parts(scale_ref[...]), axis=1).astype(bf16),
        spread_rows.astype(f32).astype(bf16),
        preferred_element_type=f32,
    )
    for b in range(blocks_here):
        place = slice(b * block_points, (b + 1) * block_points)
        factor_ref[place, :] = moments[place] * scales[b : b + 1]
    row = lax.broadcasted_iota(jnp.int32, (2 * octet, depth), 0)
    column = lax.broadcasted_iota(jnp.int32, (2 * octet, depth), 1)
    same_point = column // rows == row % octet
    part = (column % rows) // 6
    masks = [
        jnp.where(same_point & (part == 2 * h + row // octet), 1.0, 0.0).astype(bf16)
        for h in range(2)
    ]
    lane = lax.broadcasted_iota(jnp.int32, (2 * octet, bins), 1) % 4
    even, low_lane = lane % 2 == 0, lane < 2

    def shift(values, by):
        return pltpu.roll(values, by % bins, 1)

    steps_per_word, words = live_words(steps, blocks_here)
    live = [jnp.max(live_ref[word]) for word in range(words)]

    def one_block(b, carry):
        strain_copy(b).wait()
        flags = 0
        for step in range(steps):
            place = step % steps_per_word * blocks_here + b
            flags = flags | jnp.right_shift(live[step // steps_per_word], place)

        @pl.when(flags & 1 == 1)
        def _():
            place_block(b)

        return carry

    def place_block(b):
        for pair in range(block_points // (2 * octet)):
            spectra = [[], [], [], []]
            for half in range(2):
                first = pl.multiple_of(
                    b * block_points + pair * 2 * octet + half * octet, octet
                )
                here = factor_ref[pl.ds(first, octet)]
                here = jnp.concatenate([here, here], axis=0)
                coarse = here.astype(bf16)
                fine = (here - coarse.astype(f32)).astype(bf16)
                left = jnp.concatenate(
                    [coarse * masks[0], coarse * masks[1], fine * masks[0], fine * masks[1]],
                    axis=0,
                )
                own = (pair * 2 + half) * wide
                strain = strain_ref[b, own : own + depth, :]
                both = jnp.dot(left, strain, preferred_element_type=f32)
                for k in range(4):
                    spectra[k].append(
                        both[k * octet : (k + 1) * octet]
                        + both[(k + 4) * octet : (k + 5) * octet]
                    )
            green = [jnp.concatenate(s, axis=0).astype(bf16).astype(f32) for s in spectra]
            place = pl.ds(pair * 2 * octet, 2 * octet)
            below = pl.ds(block_points + pair * 2 * octet, 2 * octet)
            crossed = []
            for k in (0, 2):
                crossed.append(jnp.where(even, green[k], shift(green[k + 1], 1)))
                crossed.append(jnp.where(even, shift(green[k], -1), green[k + 1]))
            for r in range(2):
                left, right = crossed[r], crossed[r + 2]
                minus = -left
                tops = (
                    jnp.where(low_lane, left, shift(right, 2)),
                    jnp.where(low_lane, shift(left, -2), right),
                )
                bottoms = (
                    jnp.where(low_lane, right, shift(minus, 2)),
                    jnp.where(low_lane, shift(right, -2), minus),
                )
                for i in range(2):
                    out_ref[b, r + 2 * i, place, :] = tops[i].astype(bf16)
                    out_ref[b, r + 2 * i, below, :] = bottoms[i].astype(bf16)

    lax.fori_loop(0, blocks_here, one_block, 0)


def circle(cycles):
    x = cycles - jnp.round(cycles)
    z = x * x * (math.pi * math.pi)
    sine, cosine = 0.0, 0.0
    for n in range(5, -1, -1):
        sine = sine * z + (-1.0) ** n / math.factorial(2 * n + 1)
    for n in range(6, -1, -1):
        cosine = cosine * z + (-1.0) ** n / math.factorial(2 * n)
    sine = sine * x * math.pi
    return 1.0 - 2.0 * sine * sine, 2.0 * sine * cosine


def turn(a, b):
    return a[0] * b[0] - a[1] * b[1], a[0] * b[1] + a[1] * b[0]


def spectra_kernel(blocks_here, samples, first_step, onset_scale, slip_scale, live_ref, green_ref, *refs):
    steps = (len(refs) - 3) // 2
    packed, outs = refs[:steps][::-1], refs[steps : 2 * steps]
    waves, total, held = refs[-3:]
    variations, block_points = packed[0].shape[2:]
    bins = green_ref.shape[3]
    first_bin = (lax.axis_index("cmp") * bins).astype(f32)
    quarter = lax.broadcasted_iota(jnp.int32, (variations, bins), 1) // 4
    total[...] = jnp.zeros_like(total)
    for step in range(steps):
        held[step * blocks_here : (step + 1) * blocks_here] = packed[step][...]
    steps_per_word, words = live_words(first_step + steps, blocks_here)
    for word in range(words):
        flags = jnp.max(live_ref[word])
        low = max(first_step, word * steps_per_word)
        high = min(first_step + steps, (word + 1) * steps_per_word)

        def visit(place, carry):
            flag = jnp.right_shift(flags, place - word * steps_per_word * blocks_here) & 1

            @pl.when(flag == 1)
            def _():
                step = place // blocks_here
                local = place - step * blocks_here
                source = place - first_step * blocks_here
                onset = held[source, 0].astype(jnp.int32).astype(f32) + 32768.0
                slip = held[source, 1].astype(jnp.int32).astype(f32) * (1.0 / slip_scale)
                cycles = onset * (1.0 / (onset_scale * samples))
                one = circle(cycles)
                two = turn(one, one)
                four = turn(two, two)
                start = circle(cycles * first_bin)
                now = [(slip * start[0], slip * start[1])]
                now.append(turn(now[0], one))
                now.append(turn(now[0], two))
                now.append(turn(now[1], two))
                after = [turn(wave, four) for wave in now]
                double = 2.0 * four[0]
                for j in range(bins // 4):
                    rows = pl.ds(j * variations, variations)
                    for r in range(4):
                        waves[r, rows, 0:block_points] = now[r][0].astype(bf16)
                        waves[r, rows, block_points : 2 * block_points] = now[r][1].astype(bf16)
                    later = [
                        (double * after[r][0] - now[r][0], double * after[r][1] - now[r][1])
                        for r in range(4)
                    ]
                    now, after = after, later
                for r in range(4):
                    product = jnp.dot(waves[r], green_ref[local, r], preferred_element_type=f32)
                    found = product[0:variations]
                    for j in range(1, bins // 4):
                        found = jnp.where(
                            quarter == j, product[j * variations : (j + 1) * variations], found
                        )
                    total[step - first_step, r] += found

            return carry

        lax.fori_loop(low * blocks_here, high * blocks_here, visit, 0)
    for step in range(steps):
        outs[step][...] = total[step]


def spectra_call(first_step, onset_scale, slip_scale, live, green, received, name):
    steps = len(received)
    blocks_here, parts, variations, block_points = received[0].shape
    bins_here = green.shape[3]
    return pl.pallas_call(
        functools.partial(
            spectra_kernel, blocks_here, 4 * bins_here, first_step, onset_scale, slip_scale
        ),
        out_shape=[jax.ShapeDtypeStruct((4, variations, bins_here), f32)] * steps,
        in_specs=[VMEM] * (2 + steps),
        out_specs=[VMEM] * steps,
        scratch_shapes=[
            pltpu.VMEM((4, variations * bins_here // 4, 2 * block_points), bf16),
            pltpu.VMEM((steps, 4, variations, bins_here), f32),
            pltpu.VMEM((steps * blocks_here, parts, variations, block_points), jnp.int16),
        ],
        compiler_params=params(),
        cost_estimate=cost(steps * 1_000_000_000, 4_000_000 * steps),
        name=name,
    )(live, green, *received[::-1])


def three_products(left, table_high, table_low):
    rows = left.shape[0]
    coarse = left.astype(bf16)
    fine = (left - coarse.astype(f32)).astype(bf16)
    both = jnp.dot(
        jnp.concatenate([coarse, fine], axis=0), table_high, preferred_element_type=f32
    )
    return both[:rows] + both[rows:] + jnp.dot(coarse, table_low, preferred_element_type=f32)


def half_sign(bins, columns):
    odd = lax.broadcasted_iota(jnp.int32, (1, columns), 1) % bins % 2
    return (1 - 2 * odd * lax.axis_index("cmp")).astype(f32)


def band_kernel(
    bins, samples, row_ref, crossover_ref, high_ref, table_high, table_low, out_ref, weight_ref
):
    rows = jnp.concatenate([high_ref[0, :, c, :] for c in range(2)], axis=0)
    band = three_products(rows, table_high[...], table_low[...])
    sign = half_sign(bins, 2 * bins)
    out_ref[...] = -band * sign
    crossing = crossover_ref[row_ref[lax.axis_index("pt")]].astype(f32)
    column = lax.broadcasted_iota(jnp.int32, weight_ref.shape, 1) % bins
    taper = jnp.clip((crossing - column.astype(f32)) / taper_width + 0.5, 0.0, 1.0)
    weight_ref[...] = taper * (jnp.where(column == 0, 1.0, 2.0) / samples) * sign


def sum_kernel(bins_here, bins, band_ref, *refs):
    spectra, out_ref = refs[:-1], refs[-1]
    out_ref[...] = band_ref[...]
    half = lax.axis_index("cmp") * bins_here
    variations = spectra[0].shape[1]
    sums = []
    for r in range(4):
        piece = spectra[0][r]
        for other in spectra[1:]:
            piece = piece + other[r]
        sums.append(piece)
    lane = lax.broadcasted_iota(jnp.int32, (variations, bins_here), 1) % 4
    for k in range(4):
        spectrum = sums[0] if k == 0 else pltpu.roll(sums[0], bins_here - k, 1)
        for r in range(1, 4):
            moved = sums[r] if k == r else pltpu.roll(sums[r], (r - k) % bins_here, 1)
            spectrum = jnp.where(lane == r, moved, spectrum)
        place = pl.ds(pl.multiple_of((k // 2) * bins + half, bins_here), bins_here)
        rows = pl.ds((k % 2) * variations, variations)
        out_ref[rows, place] = out_ref[rows, place] + spectrum


def merge_kernel(own_ref, other_ref, weight_ref, high_ref, table_high, table_low, out_ref):
    excess = (own_ref[...] + other_ref[...]) * weight_ref[0:1]
    low = three_products(excess, table_high[...], table_low[...])
    variations = high_ref.shape[1]
    for c in range(2):
        out_ref[0, :, c, :] = high_ref[0, :, c, :] + low[c * variations : (c + 1) * variations]


def body(
    pt_size,
    strain_green,
    green_scale,
    mechanism,
    slip_amplitude,
    onset_time,
    rupture_row,
    rupture_blocks,
    block_count,
    crossover,
    high_band,
):
    points_here, strain_rows, bins_here = strain_green.shape
    blocks_here = green_scale.shape[0]
    block_points = points_here // blocks_here
    variations = slip_amplitude.shape[1]
    samples_here = high_band.shape[3]
    halves = 2
    bins = halves * bins_here
    samples = halves * samples_here
    assert slip_amplitude.shape[0] == 1 and pt_size & (pt_size - 1) == 0
    assert samples == 2 * bins and strain_rows == 24

    strain_lines = strain_green.reshape(points_here * strain_rows, bins_here)
    head_blocks = 1
    head_shape = jax.ShapeDtypeStruct((head_blocks * block_points * strain_rows, bins_here), bf16)
    pack_shape = jax.ShapeDtypeStruct((blocks_here, 2, variations, block_points), jnp.int16)
    live_shape = jax.ShapeDtypeStruct((live_words(pt_size, blocks_here)[1], 8, 128), jnp.int32)
    onset_scale, slip_scale = 512.0, 1024.0
    *packed, live, head = pl.pallas_call(
        functools.partial(pack_kernel, blocks_here, block_points, onset_scale, slip_scale),
        out_shape=[pack_shape] * pt_size + [live_shape, head_shape],
        in_specs=[HBM] * 6,
        out_specs=[VMEM] * (pt_size + 2),
        scratch_shapes=scalar_scratch((rupture_row, rupture_blocks, block_count))
        + [pltpu.VMEM(a.shape, a.dtype) for a in (slip_amplitude, onset_time)]
        + [pltpu.SemaphoreType.DMA((5,)), pltpu.SemaphoreType.DMA],
        compiler_params=params(),
        name="pack",
    )(
        *in_hbm(
            rupture_row, rupture_blocks, block_count, slip_amplitude, onset_time, strain_lines
        )
    )

    def swap(value, step):
        return lax.ppermute(value, "pt", [(i, i ^ step) for i in range(pt_size)])

    def exchange(values):
        moved = [swap(values[step], step) for step in range(pt_size - 1, 0, -1)]
        return [values[0]] + moved[::-1]

    received = exchange(packed)

    green = pl.pallas_call(
        functools.partial(green_kernel, pt_size),
        out_shape=jax.ShapeDtypeStruct((blocks_here, 4, 2 * block_points, bins_here), bf16),
        in_specs=[VMEM] * 2 + [HBM] * 3,
        out_specs=VMEM,
        scratch_shapes=[
            pltpu.VMEM((blocks_here, block_points * strain_rows + 64, bins_here), bf16),
            pltpu.VMEM((points_here, 8 * strain_rows + 64), f32),
            pltpu.VMEM(green_scale.shape, f32),
            pltpu.VMEM(mechanism.shape, f32),
            pltpu.SemaphoreType.DMA((blocks_here,)),
            pltpu.SemaphoreType.DMA((2,)),
        ],
        compiler_params=params(),
        cost_estimate=cost(2 * points_here * strain_rows * bins_here, 6_000_000),
        name="green",
    )(live, head, *in_hbm(strain_lines, green_scale, mechanism))

    sent = spectra_call(1, onset_scale, slip_scale, live, green, received[1:], "spectra")
    gathered = exchange([None] + list(sent))
    gathered[0], = spectra_call(0, onset_scale, slip_scale, live, green, received[:1], "own")

    table = fourier_table(bins, samples, samples_here)
    table_high, table_low = split_table(table)
    turned_high, turned_low = split_table(np.ascontiguousarray(table.T))
    rows = 2 * variations
    band, weight = pl.pallas_call(
        functools.partial(band_kernel, bins, samples),
        out_shape=[
            jax.ShapeDtypeStruct((rows, 2 * bins), f32),
            jax.ShapeDtypeStruct((8, 2 * bins), f32),
        ],
        in_specs=[SMEM] * 2 + [VMEM] * 3,
        out_specs=[VMEM] * 2,
        compiler_params=params(),
        cost_estimate=cost(6 * rows * samples_here * 2 * bins, 1_000_000),
        name="band",
    )(rupture_row, crossover, high_band, jnp.asarray(turned_high), jnp.asarray(turned_low))

    excess = pl.pallas_call(
        functools.partial(sum_kernel, bins_here, bins),
        out_shape=jax.ShapeDtypeStruct((rows, 2 * bins), f32),
        in_specs=[VMEM] * (1 + pt_size),
        out_specs=VMEM,
        compiler_params=params(),
        name="excess",
    )(band, *gathered[::-1])
    other = lax.ppermute(excess, "cmp", [(0, 1), (1, 0)])

    return pl.pallas_call(
        merge_kernel,
        out_shape=jax.ShapeDtypeStruct(high_band.shape, f32),
        in_specs=[VMEM] * 6,
        out_specs=VMEM,
        compiler_params=params(),
        name="merge",
    )(excess, other, weight, high_band, jnp.asarray(table_high), jnp.asarray(table_low))


def solution(mesh):
    assert mesh.shape["cmp"] == 2
    return jax.shard_map(
        functools.partial(body, mesh.shape["pt"]),
        mesh=mesh,
        in_specs=(
            P(("site", "pt"), None, "cmp"),
            P(("site", "pt"), None),
            P(None, "pt"),
            P("pt", "var", None),
            P("pt", "var", None),
            P(),
            P(),
            P(),
            P(),
            P(("site", "pt"), "var", None, "cmp"),
        ),
        out_specs=P(("site", "pt"), "var", None, "cmp"),
        check_vma=False,
    )
```

```python
import functools
import math

import jax
import jax.numpy as jnp
import ml_dtypes
import numpy as np
from jax import lax
from jax.experimental import pallas as pl
from jax.experimental.pallas import tpu as pltpu
from jax.sharding import PartitionSpec as P

taper_width = 8.0
f32 = jnp.float32
bf16 = jnp.bfloat16
highest = lax.Precision.HIGHEST
vmem_bytes = 32 * 1024 * 1024
SMEM = pl.BlockSpec(memory_space=pltpu.SMEM)
VMEM = pl.BlockSpec(memory_space=pltpu.VMEM)
HBM = pl.BlockSpec(memory_space=pltpu.HBM)


def in_hbm(*arrays):
    return [pltpu.with_memory_space_constraint(array, pltpu.HBM) for array in arrays]


def fetch(sources, targets, sems):
    copies = [
        pltpu.make_async_copy(source, target, sems.at[i])
        for i, (source, target) in enumerate(zip(sources, targets))
    ]
    for copy in copies:
        copy.start()
    return copies


def params():
    return pltpu.CompilerParams(vmem_limit_bytes=vmem_bytes)


def cost(flops, nbytes):
    return pl.CostEstimate(flops=flops, bytes_accessed=nbytes, transcendentals=0)


def split_table(table):
    high = table.astype(ml_dtypes.bfloat16)
    low = (table - high.astype(np.float64)).astype(ml_dtypes.bfloat16)
    return high, low


def fourier_table(bins, samples, samples_here):
    product = (np.arange(bins)[:, None] * np.arange(samples_here)[None, :]) % samples
    angle = product * (2.0 * np.pi / samples)
    return np.concatenate([np.cos(angle), -np.sin(angle)], axis=0)


def scalar_scratch(arrays):
    return [pltpu.SMEM(array.shape, array.dtype) for array in arrays]


def live_words(pt_size, blocks_here):
    steps_per_word = 30 // blocks_here
    return steps_per_word, pl.cdiv(pt_size, steps_per_word)


def pack_kernel(blocks_here, block_points, onset_scale, slip_scale, *refs):
    sources, later_sources, strain_hbm, outs = refs[:5], refs[5:7], refs[7], refs[8:-12]
    live_ref, head_ref, later_targets = refs[-12], refs[-11], refs[-10:-8]
    targets, sems, later_sems, head_sem = refs[-8:-3], refs[-3], refs[-2], refs[-1]
    row_ref, blocks_ref, count_ref, slip_ref, onset_ref = targets
    copies = fetch(sources, targets, sems)
    later = fetch(later_sources, later_targets, later_sems)
    head = pltpu.make_async_copy(strain_hbm.at[pl.ds(0, head_ref.shape[0])], head_ref, head_sem)
    head.start()
    later.append(head)
    for copy in copies[:3]:
        copy.wait()
    me = lax.axis_index("pt")
    rupture = row_ref[me]
    steps_per_word, words = live_words(len(outs), blocks_here)
    for word in range(words):

        def one_step(step, flags):
            other = row_ref[jnp.bitwise_xor(me, step)]

            def one_slot(slot, flags):
                local = blocks_ref[other, slot] - me * blocks_here
                bit = jnp.left_shift(1, local + (step - word * steps_per_word) * blocks_here)
                return jnp.where((local >= 0) & (local < blocks_here), flags | bit, flags)

            return lax.fori_loop(0, count_ref[other], one_slot, flags)

        last = min(len(outs), (word + 1) * steps_per_word)
        flags = lax.fori_loop(word * steps_per_word, last, one_step, 0)
        live_ref[word] = jnp.full(live_ref.shape[1:], flags, jnp.int32)
    for copy in copies[3:]:
        copy.wait()

    def visit(slot, carry):
        block = blocks_ref[rupture, slot]
        owner = block // blocks_here
        local = block - owner * blocks_here
        offset = pl.multiple_of(slot * block_points, block_points)
        onset = jnp.round(onset_ref[0, :, pl.ds(offset, block_points)] * onset_scale)
        onset = jnp.clip(onset.astype(jnp.int32) - 32768, -32768, 32767).astype(jnp.int16)
        slip = slip_ref[0, :, pl.ds(offset, block_points)].astype(f32) * slip_scale
        slip = slip.astype(jnp.int32).astype(jnp.int16)
        for step, out in enumerate(outs):

            @pl.when(owner == jnp.bitwise_xor(me, step))
            def _():
                out[local, 0] = onset
                out[local, 1] = slip

        return carry

    lax.fori_loop(0, count_ref[rupture], visit, 0)
    for copy in later:
        copy.wait()


def three_parts(values):
    parts = []
    for _ in range(3):
        parts.append(values.astype(bf16).astype(f32))
        values = values - parts[-1]
    return parts


def green_kernel(
    steps, live_ref, head_ref, strain_hbm, scale_ref, mechanism_ref, out_ref, strain_ref, factor_ref, sems
):
    rows, octet = 24, 8
    wide, depth = octet * rows, factor_ref.shape[1]
    blocks_here = scale_ref.shape[0]
    bins = strain_ref.shape[2]
    block_points = mechanism_ref.shape[1] // blocks_here
    per_block = block_points * rows

    def strain_copy(b, source=strain_hbm):
        place = pl.ds(pl.multiple_of(b * per_block, per_block), per_block)
        target = strain_ref.at[b, pl.ds(0, per_block)]
        return pltpu.make_async_copy(source.at[place], target, sems.at[b])

    for b in range(blocks_here):
        strain_copy(b, head_ref if b * per_block < head_ref.shape[0] else strain_hbm).start()
    for b in range(blocks_here):
        strain_ref[b, per_block:, :] = jnp.zeros((depth - wide, bins), bf16)
    column = lax.broadcasted_iota(jnp.int32, (18, depth), 1) % rows
    spread_six = column % 6 == lax.broadcasted_iota(jnp.int32, (18, depth), 0) % 6
    column = lax.broadcasted_iota(jnp.int32, (3 * rows, depth), 1) % rows
    spread_rows = column == lax.broadcasted_iota(jnp.int32, (3 * rows, depth), 0) % rows
    moments = lax.dot_general(
        jnp.concatenate(three_parts(mechanism_ref[...]), axis=0).astype(bf16),
        spread_six.astype(f32).astype(bf16),
        (((0,), (0,)), ((), ())),
        preferred_element_type=f32,
    )
    scales = jnp.dot(
        jnp.concatenate(three_parts(scale_ref[...]), axis=1).astype(bf16),
        spread_rows.astype(f32).astype(bf16),
        preferred_element_type=f32,
    )
    for b in range(blocks_here):
        place = slice(b * block_points, (b + 1) * block_points)
        factor_ref[place, :] = moments[place] * scales[b : b + 1]
    row = lax.broadcasted_iota(jnp.int32, (2 * octet, depth), 0)
    column = lax.broadcasted_iota(jnp.int32, (2 * octet, depth), 1)
    same_point = column // rows == row % octet
    part = (column % rows) // 6
    masks = [
        jnp.where(same_point & (part == 2 * h + row // octet), 1.0, 0.0).astype(bf16)
        for h in range(2)
    ]
    lane = lax.broadcasted_iota(jnp.int32, (2 * octet, bins), 1) % 4
    even, low_lane = lane % 2 == 0, lane < 2

    def shift(values, by):
        return pltpu.roll(values, by % bins, 1)

    steps_per_word, words = live_words(steps, blocks_here)
    live = [jnp.max(live_ref[word]) for word in range(words)]

    def one_block(b, carry):
        strain_copy(b).wait()
        flags = 0
        for step in range(steps):
            place = step % steps_per_word * blocks_here + b
            flags = flags | jnp.right_shift(live[step // steps_per_word], place)

        @pl.when(flags & 1 == 1)
        def _():
            place_block(b)

        return carry

    def place_block(b):
        for pair in range(block_points // (2 * octet)):
            spectra = [[], [], [], []]
            for half in range(2):
                first = pl.multiple_of(
                    b * block_points + pair * 2 * octet + half * octet, octet
                )
                here = factor_ref[pl.ds(first, octet)]
                here = jnp.concatenate([here, here], axis=0)
                coarse = here.astype(bf16)
                fine = (here - coarse.astype(f32)).astype(bf16)
                left = jnp.concatenate(
                    [coarse * masks[0], coarse * masks[1], fine * masks[0], fine * masks[1]],
                    axis=0,
                )
                own = (pair * 2 + half) * wide
                strain = strain_ref[b, own : own + depth, :]
                both = jnp.dot(left, strain, preferred_element_type=f32)
                for k in range(4):
                    spectra[k].append(
                        both[k * octet : (k + 1) * octet]
                        + both[(k + 4) * octet : (k + 5) * octet]
                    )
            green = [jnp.concatenate(s, axis=0).astype(bf16).astype(f32) for s in spectra]
            place = pl.ds(pair * 2 * octet, 2 * octet)
            below = pl.ds(block_points + pair * 2 * octet, 2 * octet)
            crossed = []
            for k in (0, 2):
                crossed.append(jnp.where(even, green[k], shift(green[k + 1], 1)))
                crossed.append(jnp.where(even, shift(green[k], -1), green[k + 1]))
            for r in range(2):
                left, right = crossed[r], crossed[r + 2]
                minus = -left
                tops = (
                    jnp.where(low_lane, left, shift(right, 2)),
                    jnp.where(low_lane, shift(left, -2), right),
                )
                bottoms = (
                    jnp.where(low_lane, right, shift(minus, 2)),
                    jnp.where(low_lane, shift(right, -2), minus),
                )
                for i in range(2):
                    out_ref[b, r + 2 * i, place, :] = tops[i].astype(bf16)
                    out_ref[b, r + 2 * i, below, :] = bottoms[i].astype(bf16)

    lax.fori_loop(0, blocks_here, one_block, 0)


def circle(cycles):
    x = cycles - jnp.round(cycles)
    z = x * x * (math.pi * math.pi)
    sine, cosine = 0.0, 0.0
    for n in range(5, -1, -1):
        sine = sine * z + (-1.0) ** n / math.factorial(2 * n + 1)
    for n in range(6, -1, -1):
        cosine = cosine * z + (-1.0) ** n / math.factorial(2 * n)
    sine = sine * x * math.pi
    return 1.0 - 2.0 * sine * sine, 2.0 * sine * cosine


def turn(a, b):
    return a[0] * b[0] - a[1] * b[1], a[0] * b[1] + a[1] * b[0]


def arrival_order(first_step, steps):
    return sorted(range(steps), key=lambda step: -((first_step + step) & -2))


def spectra_kernel(blocks_here, samples, first_step, onset_scale, slip_scale, live_ref, green_ref, *refs):
    steps = (len(refs) - 3) // 2
    packed, outs = refs[:steps], refs[steps : 2 * steps]
    waves, total, held = refs[-3:]
    variations, block_points = packed[0].shape[2:]
    bins = green_ref.shape[3]
    first_bin = (lax.axis_index("cmp") * bins).astype(f32)
    quarter = lax.broadcasted_iota(jnp.int32, (variations, bins), 1) // 4
    total[...] = jnp.zeros_like(total)
    for place, step in enumerate(arrival_order(first_step, steps)):
        held[step * blocks_here : (step + 1) * blocks_here] = packed[place][...]
    steps_per_word, words = live_words(first_step + steps, blocks_here)
    for word in range(words):
        flags = jnp.max(live_ref[word])
        low = max(first_step, word * steps_per_word)
        high = min(first_step + steps, (word + 1) * steps_per_word)

        def visit(place, carry):
            flag = jnp.right_shift(flags, place - word * steps_per_word * blocks_here) & 1

            @pl.when(flag == 1)
            def _():
                step = place // blocks_here
                local = place - step * blocks_here
                source = place - first_step * blocks_here
                onset = held[source, 0].astype(jnp.int32).astype(f32) + 32768.0
                slip = held[source, 1].astype(jnp.int32).astype(f32) * (1.0 / slip_scale)
                cycles = onset * (1.0 / (onset_scale * samples))
                one = circle(cycles)
                two = turn(one, one)
                four = turn(two, two)
                start = circle(cycles * first_bin)
                now = [(slip * start[0], slip * start[1])]
                now.append(turn(now[0], one))
                now.append(turn(now[0], two))
                now.append(turn(now[1], two))
                after = [turn(wave, four) for wave in now]
                double = 2.0 * four[0]
                for j in range(bins // 4):
                    rows = pl.ds(j * variations, variations)
                    for r in range(4):
                        waves[r, rows, 0:block_points] = now[r][0].astype(bf16)
                        waves[r, rows, block_points : 2 * block_points] = now[r][1].astype(bf16)
                    later = [
                        (double * after[r][0] - now[r][0], double * after[r][1] - now[r][1])
                        for r in range(4)
                    ]
                    now, after = after, later
                for r in range(4):
                    product = jnp.dot(waves[r], green_ref[local, r], preferred_element_type=f32)
                    found = product[0:variations]
                    for j in range(1, bins // 4):
                        found = jnp.where(
                            quarter == j, product[j * variations : (j + 1) * variations], found
                        )
                    total[step - first_step, r] += found

            return carry

        lax.fori_loop(low * blocks_here, high * blocks_here, visit, 0)
    for step in range(steps):
        outs[step][...] = total[step]


def spectra_call(first_step, onset_scale, slip_scale, live, green, received, name):
    steps = len(received)
    blocks_here, parts, variations, block_points = received[0].shape
    bins_here = green.shape[3]
    return pl.pallas_call(
        functools.partial(
            spectra_kernel, blocks_here, 4 * bins_here, first_step, onset_scale, slip_scale
        ),
        out_shape=[jax.ShapeDtypeStruct((4, variations, bins_here), f32)] * steps,
        in_specs=[VMEM] * (2 + steps),
        out_specs=[VMEM] * steps,
        scratch_shapes=[
            pltpu.VMEM((4, variations * bins_here // 4, 2 * block_points), bf16),
            pltpu.VMEM((steps, 4, variations, bins_here), f32),
            pltpu.VMEM((steps * blocks_here, parts, variations, block_points), jnp.int16),
        ],
        compiler_params=params(),
        cost_estimate=cost(steps * 1_000_000_000, 4_000_000 * steps),
        name=name,
    )(live, green, *[received[step] for step in arrival_order(first_step, steps)])


def three_products(left, table_high, table_low):
    rows = left.shape[0]
    coarse = left.astype(bf16)
    fine = (left - coarse.astype(f32)).astype(bf16)
    both = jnp.dot(
        jnp.concatenate([coarse, fine], axis=0), table_high, preferred_element_type=f32
    )
    return both[:rows] + both[rows:] + jnp.dot(coarse, table_low, preferred_element_type=f32)


def half_sign(bins, columns):
    odd = lax.broadcasted_iota(jnp.int32, (1, columns), 1) % bins % 2
    return (1 - 2 * odd * lax.axis_index("cmp")).astype(f32)


def band_kernel(
    bins, samples, row_ref, crossover_ref, high_ref, table_high, table_low, out_ref, weight_ref
):
    rows = jnp.concatenate([high_ref[0, :, c, :] for c in range(2)], axis=0)
    band = three_products(rows, table_high[...], table_low[...])
    sign = half_sign(bins, 2 * bins)
    out_ref[...] = -band * sign
    crossing = crossover_ref[row_ref[lax.axis_index("pt")]].astype(f32)
    column = lax.broadcasted_iota(jnp.int32, weight_ref.shape, 1) % bins
    taper = jnp.clip((crossing - column.astype(f32)) / taper_width + 0.5, 0.0, 1.0)
    weight_ref[...] = taper * (jnp.where(column == 0, 1.0, 2.0) / samples) * sign


def sum_kernel(bins_here, bins, band_ref, *refs):
    spectra, out_ref = refs[:-1], refs[-1]
    out_ref[...] = band_ref[...]
    half = lax.axis_index("cmp") * bins_here
    variations = spectra[0].shape[1]
    sums = []
    for r in range(4):
        piece = spectra[0][r]
        for other in spectra[1:]:
            piece = piece + other[r]
        sums.append(piece)
    lane = lax.broadcasted_iota(jnp.int32, (variations, bins_here), 1) % 4
    for k in range(4):
        spectrum = sums[0] if k == 0 else pltpu.roll(sums[0], bins_here - k, 1)
        for r in range(1, 4):
            moved = sums[r] if k == r else pltpu.roll(sums[r], (r - k) % bins_here, 1)
            spectrum = jnp.where(lane == r, moved, spectrum)
        place = pl.ds(pl.multiple_of((k // 2) * bins + half, bins_here), bins_here)
        rows = pl.ds((k % 2) * variations, variations)
        out_ref[rows, place] = out_ref[rows, place] + spectrum


def merge_kernel(own_ref, other_ref, weight_ref, high_ref, table_high, table_low, out_ref):
    excess = (own_ref[...] + other_ref[...]) * weight_ref[0:1]
    low = three_products(excess, table_high[...], table_low[...])
    variations = high_ref.shape[1]
    for c in range(2):
        out_ref[0, :, c, :] = high_ref[0, :, c, :] + low[c * variations : (c + 1) * variations]


def body(
    pt_size,
    strain_green,
    green_scale,
    mechanism,
    slip_amplitude,
    onset_time,
    rupture_row,
    rupture_blocks,
    block_count,
    crossover,
    high_band,
):
    points_here, strain_rows, bins_here = strain_green.shape
    blocks_here = green_scale.shape[0]
    block_points = points_here // blocks_here
    variations = slip_amplitude.shape[1]
    samples_here = high_band.shape[3]
    halves = 2
    bins = halves * bins_here
    samples = halves * samples_here
    assert slip_amplitude.shape[0] == 1 and pt_size & (pt_size - 1) == 0
    assert samples == 2 * bins and strain_rows == 24

    strain_lines = strain_green.reshape(points_here * strain_rows, bins_here)
    head_blocks = 1
    head_shape = jax.ShapeDtypeStruct((head_blocks * block_points * strain_rows, bins_here), bf16)
    pack_shape = jax.ShapeDtypeStruct((blocks_here, 2, variations, block_points), jnp.int16)
    live_shape = jax.ShapeDtypeStruct((live_words(pt_size, blocks_here)[1], 8, 128), jnp.int32)
    onset_scale, slip_scale = 512.0, 1024.0
    *packed, live, head, scale_here, mechanism_here = pl.pallas_call(
        functools.partial(pack_kernel, blocks_here, block_points, onset_scale, slip_scale),
        out_shape=[pack_shape] * pt_size
        + [live_shape, head_shape]
        + [jax.ShapeDtypeStruct(a.shape, a.dtype) for a in (green_scale, mechanism)],
        in_specs=[HBM] * 8,
        out_specs=[VMEM] * (pt_size + 4),
        scratch_shapes=scalar_scratch((rupture_row, rupture_blocks, block_count))
        + [pltpu.VMEM(a.shape, a.dtype) for a in (slip_amplitude, onset_time)]
        + [
            pltpu.SemaphoreType.DMA((5,)),
            pltpu.SemaphoreType.DMA((2,)),
            pltpu.SemaphoreType.DMA,
        ],
        compiler_params=params(),
        name="pack",
    )(
        *in_hbm(
            rupture_row,
            rupture_blocks,
            block_count,
            slip_amplitude,
            onset_time,
            green_scale,
            mechanism,
            strain_lines,
        )
    )

    def swap(value, step):
        return lax.ppermute(value, "pt", [(i, i ^ step) for i in range(pt_size)])

    def exchange(values):
        moved = [swap(values[step], step) for step in range(pt_size - 1, 0, -1)]
        return [values[0]] + moved[::-1]

    received = exchange(packed)

    green = pl.pallas_call(
        functools.partial(green_kernel, pt_size),
        out_shape=jax.ShapeDtypeStruct((blocks_here, 4, 2 * block_points, bins_here), bf16),
        in_specs=[VMEM] * 2 + [HBM] + [VMEM] * 2,
        out_specs=VMEM,
        scratch_shapes=[
            pltpu.VMEM((blocks_here, block_points * strain_rows + 64, bins_here), bf16),
            pltpu.VMEM((points_here, 8 * strain_rows + 64), f32),
            pltpu.SemaphoreType.DMA((blocks_here,)),
        ],
        compiler_params=params(),
        cost_estimate=cost(2 * points_here * strain_rows * bins_here, 6_000_000),
        name="green",
    )(live, head, *in_hbm(strain_lines), scale_here, mechanism_here)

    sent = spectra_call(1, onset_scale, slip_scale, live, green, received[1:], "spectra")
    gathered = exchange([None] + list(sent))
    gathered[0], = spectra_call(0, onset_scale, slip_scale, live, green, received[:1], "own")

    table = fourier_table(bins, samples, samples_here)
    table_high, table_low = split_table(table)
    turned_high, turned_low = split_table(np.ascontiguousarray(table.T))
    rows = 2 * variations
    band, weight = pl.pallas_call(
        functools.partial(band_kernel, bins, samples),
        out_shape=[
            jax.ShapeDtypeStruct((rows, 2 * bins), f32),
            jax.ShapeDtypeStruct((8, 2 * bins), f32),
        ],
        in_specs=[SMEM] * 2 + [VMEM] * 3,
        out_specs=[VMEM] * 2,
        compiler_params=params(),
        cost_estimate=cost(6 * rows * samples_here * 2 * bins, 1_000_000),
        name="band",
    )(rupture_row, crossover, high_band, jnp.asarray(turned_high), jnp.asarray(turned_low))

    excess = pl.pallas_call(
        functools.partial(sum_kernel, bins_here, bins),
        out_shape=jax.ShapeDtypeStruct((rows, 2 * bins), f32),
        in_specs=[VMEM] * (1 + pt_size),
        out_specs=VMEM,
        compiler_params=params(),
        name="excess",
    )(band, *gathered[::-1])
    other = lax.ppermute(excess, "cmp", [(0, 1), (1, 0)])

    return pl.pallas_call(
        merge_kernel,
        out_shape=jax.ShapeDtypeStruct(high_band.shape, f32),
        in_specs=[VMEM] * 6,
        out_specs=VMEM,
        compiler_params=params(),
        name="merge",
    )(excess, other, weight, high_band, jnp.asarray(table_high), jnp.asarray(table_low))


def solution(mesh):
    assert mesh.shape["cmp"] == 2
    return jax.shard_map(
        functools.partial(body, mesh.shape["pt"]),
        mesh=mesh,
        in_specs=(
            P(("site", "pt"), None, "cmp"),
            P(("site", "pt"), None),
            P(None, "pt"),
            P("pt", "var", None),
            P("pt", "var", None),
            P(),
            P(),
            P(),
            P(),
            P(("site", "pt"), "var", None, "cmp"),
        ),
        out_specs=P(("site", "pt"), "var", None, "cmp"),
        check_vma=False,
    )
```

```python
import functools
import math

import jax
import jax.numpy as jnp
import ml_dtypes
import numpy as np
from jax import lax
from jax.experimental import pallas as pl
from jax.experimental.pallas import tpu as pltpu
from jax.sharding import PartitionSpec as P

taper_width = 8.0
f32 = jnp.float32
bf16 = jnp.bfloat16
highest = lax.Precision.HIGHEST
vmem_bytes = 32 * 1024 * 1024
SMEM = pl.BlockSpec(memory_space=pltpu.SMEM)
VMEM = pl.BlockSpec(memory_space=pltpu.VMEM)
HBM = pl.BlockSpec(memory_space=pltpu.HBM)


def in_hbm(*arrays):
    return [pltpu.with_memory_space_constraint(array, pltpu.HBM) for array in arrays]


def fetch(sources, targets, sems):
    copies = [
        pltpu.make_async_copy(source, target, sems.at[i])
        for i, (source, target) in enumerate(zip(sources, targets))
    ]
    for copy in copies:
        copy.start()
    return copies


def params():
    return pltpu.CompilerParams(vmem_limit_bytes=vmem_bytes)


def cost(flops, nbytes):
    return pl.CostEstimate(flops=flops, bytes_accessed=nbytes, transcendentals=0)


def split_table(table):
    high = table.astype(ml_dtypes.bfloat16)
    low = (table - high.astype(np.float64)).astype(ml_dtypes.bfloat16)
    return high, low


def fourier_table(bins, samples, samples_here):
    product = (np.arange(bins)[:, None] * np.arange(samples_here)[None, :]) % samples
    angle = product * (2.0 * np.pi / samples)
    return np.concatenate([np.cos(angle), -np.sin(angle)], axis=0)


def scalar_scratch(arrays):
    return [pltpu.SMEM(array.shape, array.dtype) for array in arrays]


def live_words(pt_size, blocks_here):
    steps_per_word = 30 // blocks_here
    return steps_per_word, pl.cdiv(pt_size, steps_per_word)


def pack_kernel(blocks_here, block_points, onset_scale, slip_scale, *refs):
    sources, later_sources, strain_hbm, outs = refs[:5], refs[5:7], refs[7], refs[8:-13]
    live_ref, head_ref, later_targets = refs[-13], refs[-12], refs[-11:-9]
    targets, coded, sems, later_sems, head_sem = refs[-9:-4], *refs[-4:]
    row_ref, blocks_ref, count_ref, slip_ref, onset_ref = targets
    copies = fetch(sources, targets, sems)
    later = fetch(later_sources, later_targets, later_sems)
    head = pltpu.make_async_copy(strain_hbm.at[pl.ds(0, head_ref.shape[0])], head_ref, head_sem)
    head.start()
    later.append(head)
    for copy in copies[:3]:
        copy.wait()
    me = lax.axis_index("pt")
    rupture = row_ref[me]
    steps_per_word, words = live_words(len(outs), blocks_here)
    for word in range(words):

        def one_step(step, flags):
            other = row_ref[jnp.bitwise_xor(me, step)]

            def one_slot(slot, flags):
                local = blocks_ref[other, slot] - me * blocks_here
                bit = jnp.left_shift(1, local + (step - word * steps_per_word) * blocks_here)
                return jnp.where((local >= 0) & (local < blocks_here), flags | bit, flags)

            return lax.fori_loop(0, count_ref[other], one_slot, flags)

        last = min(len(outs), (word + 1) * steps_per_word)
        flags = lax.fori_loop(word * steps_per_word, last, one_step, 0)
        live_ref[word] = jnp.full(live_ref.shape[1:], flags, jnp.int32)
    for copy in copies[3:]:
        copy.wait()

    def visit(slot, carry):
        block = blocks_ref[rupture, slot]
        owner = block // blocks_here
        local = block - owner * blocks_here
        offset = pl.multiple_of(slot * block_points, block_points)
        onset = jnp.round(onset_ref[0, :, pl.ds(offset, block_points)] * onset_scale)
        onset = jnp.clip(onset.astype(jnp.int32) - 32768, -32768, 32767).astype(jnp.int16)
        slip = slip_ref[0, :, pl.ds(offset, block_points)].astype(f32) * slip_scale
        slip = slip.astype(jnp.int32).astype(jnp.int16)
        place = jnp.bitwise_xor(me, owner) * blocks_here + local
        coded[place, 0] = onset
        coded[place, 1] = slip
        return carry

    lax.fori_loop(0, count_ref[rupture], visit, 0)
    for step, out in enumerate(outs):
        out[...] = coded[step * blocks_here : (step + 1) * blocks_here]
    for copy in later:
        copy.wait()


def three_parts(values):
    parts = []
    for _ in range(3):
        parts.append(values.astype(bf16).astype(f32))
        values = values - parts[-1]
    return parts


def green_kernel(
    steps, live_ref, head_ref, strain_hbm, scale_ref, mechanism_ref, out_ref, strain_ref, factor_ref, sems
):
    rows, octet = 24, 8
    wide, depth = octet * rows, factor_ref.shape[1]
    blocks_here = scale_ref.shape[0]
    bins = strain_ref.shape[2]
    block_points = mechanism_ref.shape[1] // blocks_here
    per_block = block_points * rows

    def strain_copy(b, source=strain_hbm):
        place = pl.ds(pl.multiple_of(b * per_block, per_block), per_block)
        target = strain_ref.at[b, pl.ds(0, per_block)]
        return pltpu.make_async_copy(source.at[place], target, sems.at[b])

    for b in range(blocks_here):
        strain_copy(b, head_ref if b * per_block < head_ref.shape[0] else strain_hbm).start()
    for b in range(blocks_here):
        strain_ref[b, per_block:, :] = jnp.zeros((depth - wide, bins), bf16)
    column = lax.broadcasted_iota(jnp.int32, (18, depth), 1) % rows
    spread_six = column % 6 == lax.broadcasted_iota(jnp.int32, (18, depth), 0) % 6
    column = lax.broadcasted_iota(jnp.int32, (3 * rows, depth), 1) % rows
    spread_rows = column == lax.broadcasted_iota(jnp.int32, (3 * rows, depth), 0) % rows
    moments = lax.dot_general(
        jnp.concatenate(three_parts(mechanism_ref[...]), axis=0).astype(bf16),
        spread_six.astype(f32).astype(bf16),
        (((0,), (0,)), ((), ())),
        preferred_element_type=f32,
    )
    scales = jnp.dot(
        jnp.concatenate(three_parts(scale_ref[...]), axis=1).astype(bf16),
        spread_rows.astype(f32).astype(bf16),
        preferred_element_type=f32,
    )
    for b in range(blocks_here):
        place = slice(b * block_points, (b + 1) * block_points)
        factor_ref[place, :] = moments[place] * scales[b : b + 1]
    row = lax.broadcasted_iota(jnp.int32, (2 * octet, depth), 0)
    column = lax.broadcasted_iota(jnp.int32, (2 * octet, depth), 1)
    same_point = column // rows == row % octet
    part = (column % rows) // 6
    masks = [
        jnp.where(same_point & (part == 2 * h + row // octet), 1.0, 0.0).astype(bf16)
        for h in range(2)
    ]
    lane = lax.broadcasted_iota(jnp.int32, (2 * octet, bins), 1) % 4
    even, low_lane = lane % 2 == 0, lane < 2

    def shift(values, by):
        return pltpu.roll(values, by % bins, 1)

    steps_per_word, words = live_words(steps, blocks_here)
    live = [jnp.max(live_ref[word]) for word in range(words)]

    def one_block(b, carry):
        strain_copy(b).wait()
        flags = 0
        for step in range(steps):
            place = step % steps_per_word * blocks_here + b
            flags = flags | jnp.right_shift(live[step // steps_per_word], place)

        @pl.when(flags & 1 == 1)
        def _():
            place_block(b)

        return carry

    def place_block(b):
        for pair in range(block_points // (2 * octet)):
            spectra = [[], [], [], []]
            for half in range(2):
                first = pl.multiple_of(
                    b * block_points + pair * 2 * octet + half * octet, octet
                )
                here = factor_ref[pl.ds(first, octet)]
                here = jnp.concatenate([here, here], axis=0)
                coarse = here.astype(bf16)
                fine = (here - coarse.astype(f32)).astype(bf16)
                left = jnp.concatenate(
                    [coarse * masks[0], coarse * masks[1], fine * masks[0], fine * masks[1]],
                    axis=0,
                )
                own = (pair * 2 + half) * wide
                strain = strain_ref[b, own : own + depth, :]
                both = jnp.dot(left, strain, preferred_element_type=f32)
                for k in range(4):
                    spectra[k].append(
                        both[k * octet : (k + 1) * octet]
                        + both[(k + 4) * octet : (k + 5) * octet]
                    )
            green = [jnp.concatenate(s, axis=0).astype(bf16).astype(f32) for s in spectra]
            place = pl.ds(pair * 2 * octet, 2 * octet)
            below = pl.ds(block_points + pair * 2 * octet, 2 * octet)
            crossed = []
            for k in (0, 2):
                crossed.append(jnp.where(even, green[k], shift(green[k + 1], 1)))
                crossed.append(jnp.where(even, shift(green[k], -1), green[k + 1]))
            for r in range(2):
                left, right = crossed[r], crossed[r + 2]
                minus = -left
                tops = (
                    jnp.where(low_lane, left, shift(right, 2)),
                    jnp.where(low_lane, shift(left, -2), right),
                )
                bottoms = (
                    jnp.where(low_lane, right, shift(minus, 2)),
                    jnp.where(low_lane, shift(right, -2), minus),
                )
                for i in range(2):
                    out_ref[b, r + 2 * i, place, :] = tops[i].astype(bf16)
                    out_ref[b, r + 2 * i, below, :] = bottoms[i].astype(bf16)

    lax.fori_loop(0, blocks_here, one_block, 0)


def circle(cycles):
    x = cycles - jnp.round(cycles)
    z = x * x * (math.pi * math.pi)
    sine, cosine = 0.0, 0.0
    for n in range(5, -1, -1):
        sine = sine * z + (-1.0) ** n / math.factorial(2 * n + 1)
    for n in range(6, -1, -1):
        cosine = cosine * z + (-1.0) ** n / math.factorial(2 * n)
    sine = sine * x * math.pi
    return 1.0 - 2.0 * sine * sine, 2.0 * sine * cosine


def turn(a, b):
    return a[0] * b[0] - a[1] * b[1], a[0] * b[1] + a[1] * b[0]


def arrival_order(first_step, steps):
    return sorted(range(steps), key=lambda step: -((first_step + step) & -2))


def spectra_kernel(blocks_here, samples, first_step, onset_scale, slip_scale, live_ref, green_ref, *refs):
    steps = (len(refs) - 3) // 2
    packed, outs = refs[:steps], refs[steps : 2 * steps]
    waves, total, held = refs[-3:]
    variations, block_points = packed[0].shape[2:]
    bins = green_ref.shape[3]
    first_bin = (lax.axis_index("cmp") * bins).astype(f32)
    quarter = lax.broadcasted_iota(jnp.int32, (variations, bins), 1) // 4
    total[...] = jnp.zeros_like(total)
    for place, step in enumerate(arrival_order(first_step, steps)):
        held[step * blocks_here : (step + 1) * blocks_here] = packed[place][...]
    steps_per_word, words = live_words(first_step + steps, blocks_here)
    for word in range(words):
        flags = jnp.max(live_ref[word])
        low = max(first_step, word * steps_per_word)
        high = min(first_step + steps, (word + 1) * steps_per_word)

        def visit(left):
            bit = 31 - lax.clz(left)
            place = bit + word * steps_per_word * blocks_here
            step = place // blocks_here
            local = place - step * blocks_here
            source = place - first_step * blocks_here
            onset = held[source, 0].astype(jnp.int32).astype(f32) + 32768.0
            slip = held[source, 1].astype(jnp.int32).astype(f32) * (1.0 / slip_scale)
            cycles = onset * (1.0 / (onset_scale * samples))
            one = circle(cycles)
            two = turn(one, one)
            four = turn(two, two)
            start = circle(cycles * first_bin)
            now = [(slip * start[0], slip * start[1])]
            now.append(turn(now[0], one))
            now.append(turn(now[0], two))
            now.append(turn(now[1], two))
            after = [turn(wave, four) for wave in now]
            double = 2.0 * four[0]
            for j in range(bins // 4):
                rows = pl.ds(j * variations, variations)
                for r in range(4):
                    waves[r, rows, 0:block_points] = now[r][0].astype(bf16)
                    waves[r, rows, block_points : 2 * block_points] = now[r][1].astype(bf16)
                later = [
                    (double * after[r][0] - now[r][0], double * after[r][1] - now[r][1])
                    for r in range(4)
                ]
                now, after = after, later
            for r in range(4):
                product = jnp.dot(waves[r], green_ref[local, r], preferred_element_type=f32)
                found = product[0:variations]
                for j in range(1, bins // 4):
                    found = jnp.where(
                        quarter == j, product[j * variations : (j + 1) * variations], found
                    )
                total[step - first_step, r] += found

            return left ^ jnp.left_shift(1, bit)

        first = (low - word * steps_per_word) * blocks_here
        last = (high - word * steps_per_word) * blocks_here
        flags = flags & ((1 << last) - (1 << first))
        lax.while_loop(lambda left: left != 0, visit, flags)
    for step in range(steps):
        outs[step][...] = total[step]


def spectra_call(first_step, onset_scale, slip_scale, live, green, received, name):
    steps = len(received)
    blocks_here, parts, variations, block_points = received[0].shape
    bins_here = green.shape[3]
    return pl.pallas_call(
        functools.partial(
            spectra_kernel, blocks_here, 4 * bins_here, first_step, onset_scale, slip_scale
        ),
        out_shape=[jax.ShapeDtypeStruct((4, variations, bins_here), f32)] * steps,
        in_specs=[VMEM] * (2 + steps),
        out_specs=[VMEM] * steps,
        scratch_shapes=[
            pltpu.VMEM((4, variations * bins_here // 4, 2 * block_points), bf16),
            pltpu.VMEM((steps, 4, variations, bins_here), f32),
            pltpu.VMEM((steps * blocks_here, parts, variations, block_points), jnp.int16),
        ],
        compiler_params=params(),
        cost_estimate=cost(steps * 1_000_000_000, 4_000_000 * steps),
        name=name,
    )(live, green, *[received[step] for step in arrival_order(first_step, steps)])


def three_products(left, table_high, table_low):
    rows = left.shape[0]
    coarse = left.astype(bf16)
    fine = (left - coarse.astype(f32)).astype(bf16)
    both = jnp.dot(
        jnp.concatenate([coarse, fine], axis=0), table_high, preferred_element_type=f32
    )
    return both[:rows] + both[rows:] + jnp.dot(coarse, table_low, preferred_element_type=f32)


def half_sign(bins, columns):
    odd = lax.broadcasted_iota(jnp.int32, (1, columns), 1) % bins % 2
    return (1 - 2 * odd * lax.axis_index("cmp")).astype(f32)


def band_kernel(
    bins, samples, row_ref, crossover_ref, high_ref, table_high, table_low, out_ref, weight_ref
):
    rows = jnp.concatenate([high_ref[0, :, c, :] for c in range(2)], axis=0)
    band = three_products(rows, table_high[...], table_low[...])
    sign = half_sign(bins, 2 * bins)
    out_ref[...] = -band * sign
    crossing = crossover_ref[row_ref[lax.axis_index("pt")]].astype(f32)
    column = lax.broadcasted_iota(jnp.int32, weight_ref.shape, 1) % bins
    taper = jnp.clip((crossing - column.astype(f32)) / taper_width + 0.5, 0.0, 1.0)
    weight_ref[...] = taper * (jnp.where(column == 0, 1.0, 2.0) / samples) * sign


def sum_kernel(bins_here, bins, band_ref, *refs):
    spectra, out_ref = refs[:-1], refs[-1]
    out_ref[...] = band_ref[...]
    half = lax.axis_index("cmp") * bins_here
    variations = spectra[0].shape[1]
    sums = []
    for r in range(4):
        piece = spectra[0][r]
        for other in spectra[1:]:
            piece = piece + other[r]
        sums.append(piece)
    lane = lax.broadcasted_iota(jnp.int32, (variations, bins_here), 1) % 4
    for k in range(4):
        spectrum = sums[0] if k == 0 else pltpu.roll(sums[0], bins_here - k, 1)
        for r in range(1, 4):
            moved = sums[r] if k == r else pltpu.roll(sums[r], (r - k) % bins_here, 1)
            spectrum = jnp.where(lane == r, moved, spectrum)
        place = pl.ds(pl.multiple_of((k // 2) * bins + half, bins_here), bins_here)
        rows = pl.ds((k % 2) * variations, variations)
        out_ref[rows, place] = out_ref[rows, place] + spectrum


def merge_kernel(own_ref, other_ref, weight_ref, high_ref, table_high, table_low, out_ref):
    excess = (own_ref[...] + other_ref[...]) * weight_ref[0:1]
    low = three_products(excess, table_high[...], table_low[...])
    variations = high_ref.shape[1]
    for c in range(2):
        out_ref[0, :, c, :] = high_ref[0, :, c, :] + low[c * variations : (c + 1) * variations]


def body(
    pt_size,
    strain_green,
    green_scale,
    mechanism,
    slip_amplitude,
    onset_time,
    rupture_row,
    rupture_blocks,
    block_count,
    crossover,
    high_band,
):
    points_here, strain_rows, bins_here = strain_green.shape
    blocks_here = green_scale.shape[0]
    block_points = points_here // blocks_here
    variations = slip_amplitude.shape[1]
    samples_here = high_band.shape[3]
    halves = 2
    bins = halves * bins_here
    samples = halves * samples_here
    assert slip_amplitude.shape[0] == 1 and pt_size & (pt_size - 1) == 0
    assert samples == 2 * bins and strain_rows == 24

    strain_lines = strain_green.reshape(points_here * strain_rows, bins_here)
    head_blocks = 1
    head_shape = jax.ShapeDtypeStruct((head_blocks * block_points * strain_rows, bins_here), bf16)
    pack_shape = jax.ShapeDtypeStruct((blocks_here, 2, variations, block_points), jnp.int16)
    live_shape = jax.ShapeDtypeStruct((live_words(pt_size, blocks_here)[1], 8, 128), jnp.int32)
    onset_scale, slip_scale = 512.0, 1024.0
    *packed, live, head, scale_here, mechanism_here = pl.pallas_call(
        functools.partial(pack_kernel, blocks_here, block_points, onset_scale, slip_scale),
        out_shape=[pack_shape] * pt_size
        + [live_shape, head_shape]
        + [jax.ShapeDtypeStruct(a.shape, a.dtype) for a in (green_scale, mechanism)],
        in_specs=[HBM] * 8,
        out_specs=[VMEM] * (pt_size + 4),
        scratch_shapes=scalar_scratch((rupture_row, rupture_blocks, block_count))
        + [pltpu.VMEM(a.shape, a.dtype) for a in (slip_amplitude, onset_time)]
        + [
            pltpu.VMEM((pt_size * blocks_here,) + pack_shape.shape[1:], jnp.int16),
            pltpu.SemaphoreType.DMA((5,)),
            pltpu.SemaphoreType.DMA((2,)),
            pltpu.SemaphoreType.DMA,
        ],
        compiler_params=params(),
        name="pack",
    )(
        *in_hbm(
            rupture_row,
            rupture_blocks,
            block_count,
            slip_amplitude,
            onset_time,
            green_scale,
            mechanism,
            strain_lines,
        )
    )

    def swap(value, step):
        return lax.ppermute(value, "pt", [(i, i ^ step) for i in range(pt_size)])

    def exchange(values):
        moved = [swap(values[step], step) for step in range(pt_size - 1, 0, -1)]
        return [values[0]] + moved[::-1]

    received = exchange(packed)

    green = pl.pallas_call(
        functools.partial(green_kernel, pt_size),
        out_shape=jax.ShapeDtypeStruct((blocks_here, 4, 2 * block_points, bins_here), bf16),
        in_specs=[VMEM] * 2 + [HBM] + [VMEM] * 2,
        out_specs=VMEM,
        scratch_shapes=[
            pltpu.VMEM((blocks_here, block_points * strain_rows + 64, bins_here), bf16),
            pltpu.VMEM((points_here, 8 * strain_rows + 64), f32),
            pltpu.SemaphoreType.DMA((blocks_here,)),
        ],
        compiler_params=params(),
        cost_estimate=cost(2 * points_here * strain_rows * bins_here, 6_000_000),
        name="green",
    )(live, head, *in_hbm(strain_lines), scale_here, mechanism_here)

    sent = spectra_call(1, onset_scale, slip_scale, live, green, received[1:], "spectra")
    gathered = exchange([None] + list(sent))
    gathered[0], = spectra_call(0, onset_scale, slip_scale, live, green, received[:1], "own")

    table = fourier_table(bins, samples, samples_here)
    table_high, table_low = split_table(table)
    turned_high, turned_low = split_table(np.ascontiguousarray(table.T))
    rows = 2 * variations
    band, weight = pl.pallas_call(
        functools.partial(band_kernel, bins, samples),
        out_shape=[
            jax.ShapeDtypeStruct((rows, 2 * bins), f32),
            jax.ShapeDtypeStruct((8, 2 * bins), f32),
        ],
        in_specs=[SMEM] * 2 + [VMEM] * 3,
        out_specs=[VMEM] * 2,
        compiler_params=params(),
        cost_estimate=cost(6 * rows * samples_here * 2 * bins, 1_000_000),
        name="band",
    )(rupture_row, crossover, high_band, jnp.asarray(turned_high), jnp.asarray(turned_low))

    excess = pl.pallas_call(
        functools.partial(sum_kernel, bins_here, bins),
        out_shape=jax.ShapeDtypeStruct((rows, 2 * bins), f32),
        in_specs=[VMEM] * (1 + pt_size),
        out_specs=VMEM,
        compiler_params=params(),
        name="excess",
    )(band, *gathered[::-1])
    other = lax.ppermute(excess, "cmp", [(0, 1), (1, 0)])

    return pl.pallas_call(
        merge_kernel,
        out_shape=jax.ShapeDtypeStruct(high_band.shape, f32),
        in_specs=[VMEM] * 6,
        out_specs=VMEM,
        compiler_params=params(),
        name="merge",
    )(excess, other, weight, high_band, jnp.asarray(table_high), jnp.asarray(table_low))


def solution(mesh):
    assert mesh.shape["cmp"] == 2
    return jax.shard_map(
        functools.partial(body, mesh.shape["pt"]),
        mesh=mesh,
        in_specs=(
            P(("site", "pt"), None, "cmp"),
            P(("site", "pt"), None),
            P(None, "pt"),
            P("pt", "var", None),
            P("pt", "var", None),
            P(),
            P(),
            P(),
            P(),
            P(("site", "pt"), "var", None, "cmp"),
        ),
        out_specs=P(("site", "pt"), "var", None, "cmp"),
        check_vma=False,
    )
```

```python
import functools
import math

import jax
import jax.numpy as jnp
import ml_dtypes
import numpy as np
from jax import lax
from jax.experimental import pallas as pl
from jax.experimental.pallas import tpu as pltpu
from jax.sharding import PartitionSpec as P

taper_width = 8.0
f32 = jnp.float32
bf16 = jnp.bfloat16
highest = lax.Precision.HIGHEST
vmem_bytes = 32 * 1024 * 1024
SMEM = pl.BlockSpec(memory_space=pltpu.SMEM)
VMEM = pl.BlockSpec(memory_space=pltpu.VMEM)
HBM = pl.BlockSpec(memory_space=pltpu.HBM)


def in_hbm(*arrays):
    return [pltpu.with_memory_space_constraint(array, pltpu.HBM) for array in arrays]


def fetch(sources, targets, sems):
    copies = [
        pltpu.make_async_copy(source, target, sems.at[i])
        for i, (source, target) in enumerate(zip(sources, targets))
    ]
    for copy in copies:
        copy.start()
    return copies


def params():
    return pltpu.CompilerParams(vmem_limit_bytes=vmem_bytes)


def cost(flops, nbytes):
    return pl.CostEstimate(flops=flops, bytes_accessed=nbytes, transcendentals=0)


def split_table(table):
    high = table.astype(ml_dtypes.bfloat16)
    low = (table - high.astype(np.float64)).astype(ml_dtypes.bfloat16)
    return high, low


def fourier_table(bins, samples, samples_here):
    product = (np.arange(bins)[:, None] * np.arange(samples_here)[None, :]) % samples
    angle = product * (2.0 * np.pi / samples)
    return np.concatenate([np.cos(angle), -np.sin(angle)], axis=0)


def scalar_scratch(arrays):
    return [pltpu.SMEM(array.shape, array.dtype) for array in arrays]


def live_words(pt_size, blocks_here):
    steps_per_word = 30 // blocks_here
    return steps_per_word, pl.cdiv(pt_size, steps_per_word)


def pack_kernel(blocks_here, block_points, onset_scale, slip_scale, *refs):
    sources, later_sources, outs = refs[:5], refs[5:7], refs[8:-11]
    live_ref, later_targets = refs[-11], refs[-10:-8]
    targets, coded, sems, later_sems = refs[-8:-3], *refs[-3:]
    row_ref, blocks_ref, count_ref, slip_ref, onset_ref = targets
    copies = fetch(sources, targets, sems)
    later = fetch(later_sources, later_targets, later_sems)
    for copy in copies[:3]:
        copy.wait()
    me = lax.axis_index("pt")
    rupture = row_ref[me]
    steps_per_word, words = live_words(len(outs), blocks_here)
    for word in range(words):

        def one_step(step, flags):
            other = row_ref[jnp.bitwise_xor(me, step)]

            def one_slot(slot, flags):
                local = blocks_ref[other, slot] - me * blocks_here
                bit = jnp.left_shift(1, local + (step - word * steps_per_word) * blocks_here)
                return jnp.where((local >= 0) & (local < blocks_here), flags | bit, flags)

            return lax.fori_loop(0, count_ref[other], one_slot, flags)

        last = min(len(outs), (word + 1) * steps_per_word)
        flags = lax.fori_loop(word * steps_per_word, last, one_step, 0)
        live_ref[word] = jnp.full(live_ref.shape[1:], flags, jnp.int32)
    for copy in copies[3:]:
        copy.wait()

    def visit(slot, carry):
        block = blocks_ref[rupture, slot]
        owner = block // blocks_here
        local = block - owner * blocks_here
        offset = pl.multiple_of(slot * block_points, block_points)
        onset = jnp.round(onset_ref[0, :, pl.ds(offset, block_points)] * onset_scale)
        onset = jnp.clip(onset.astype(jnp.int32) - 32768, -32768, 32767).astype(jnp.int16)
        slip = slip_ref[0, :, pl.ds(offset, block_points)].astype(f32) * slip_scale
        slip = slip.astype(jnp.int32).astype(jnp.int16)
        place = jnp.bitwise_xor(me, owner) * blocks_here + local
        coded[place, 0] = onset
        coded[place, 1] = slip
        return carry

    lax.fori_loop(0, count_ref[rupture], visit, 0)
    for step, out in enumerate(outs):
        out[...] = coded[step * blocks_here : (step + 1) * blocks_here]
    for copy in later:
        copy.wait()


def three_parts(values):
    parts = []
    for _ in range(3):
        parts.append(values.astype(bf16).astype(f32))
        values = values - parts[-1]
    return parts


def green_kernel(
    steps, live_ref, strain_ref, scale_ref, mechanism_ref, out_ref, factor_ref
):
    rows, octet = 24, 8
    wide, depth = octet * rows, factor_ref.shape[1]
    blocks_here = scale_ref.shape[0]
    bins = strain_ref.shape[1]
    block_points = mechanism_ref.shape[1] // blocks_here
    per_block = block_points * rows

    column = lax.broadcasted_iota(jnp.int32, (18, depth), 1) % rows
    spread_six = column % 6 == lax.broadcasted_iota(jnp.int32, (18, depth), 0) % 6
    column = lax.broadcasted_iota(jnp.int32, (3 * rows, depth), 1) % rows
    spread_rows = column == lax.broadcasted_iota(jnp.int32, (3 * rows, depth), 0) % rows
    moments = lax.dot_general(
        jnp.concatenate(three_parts(mechanism_ref[...]), axis=0).astype(bf16),
        spread_six.astype(f32).astype(bf16),
        (((0,), (0,)), ((), ())),
        preferred_element_type=f32,
    )
    scales = jnp.dot(
        jnp.concatenate(three_parts(scale_ref[...]), axis=1).astype(bf16),
        spread_rows.astype(f32).astype(bf16),
        preferred_element_type=f32,
    )
    for b in range(blocks_here):
        place = slice(b * block_points, (b + 1) * block_points)
        factor_ref[place, :] = moments[place] * scales[b : b + 1]
    row = lax.broadcasted_iota(jnp.int32, (2 * octet, depth), 0)
    column = lax.broadcasted_iota(jnp.int32, (2 * octet, depth), 1)

    def point_masks(first_column):
        place = column - first_column
        mine = (place // rows == row % octet) & (place >= 0)
        part = (place % rows) // 6
        return [
            jnp.where(mine & (part == 2 * h + row // octet), 1.0, 0.0).astype(bf16)
            for h in range(2)
        ]

    spare = depth - wide
    usual, at_end = point_masks(0), point_masks(spare)
    lane = lax.broadcasted_iota(jnp.int32, (2 * octet, bins), 1) % 4
    even, low_lane = lane % 2 == 0, lane < 2

    def shift(values, by):
        return pltpu.roll(values, by % bins, 1)

    steps_per_word, words = live_words(steps, blocks_here)
    live = [jnp.max(live_ref[word]) for word in range(words)]

    def one_block(b, carry):
        flags = 0
        for step in range(steps):
            place = step % steps_per_word * blocks_here + b
            flags = flags | jnp.right_shift(live[step // steps_per_word], place)

        @pl.when(flags & 1 == 1)
        def _():
            place_block(b)

        return carry

    def place_block(b):
        for pair in range(block_points // (2 * octet)):
            spectra = [[], [], [], []]
            for half in range(2):
                first = pl.multiple_of(
                    b * block_points + pair * 2 * octet + half * octet, octet
                )
                here = factor_ref[pl.ds(first, octet)]
                last = (pair + 1) * 2 * octet == block_points and half == 1
                masks = at_end if last else usual
                if last:
                    here = pltpu.roll(here, spare, 1)
                here = jnp.concatenate([here, here], axis=0)
                coarse = here.astype(bf16)
                fine = (here - coarse.astype(f32)).astype(bf16)
                left = jnp.concatenate(
                    [coarse * masks[0], coarse * masks[1], fine * masks[0], fine * masks[1]],
                    axis=0,
                )
                begin = pl.multiple_of(first * rows - (spare if last else 0), 64)
                strain = strain_ref[pl.ds(begin, depth), :]
                both = jnp.dot(left, strain, preferred_element_type=f32)
                for k in range(4):
                    spectra[k].append(
                        both[k * octet : (k + 1) * octet]
                        + both[(k + 4) * octet : (k + 5) * octet]
                    )
            green = [jnp.concatenate(s, axis=0).astype(bf16).astype(f32) for s in spectra]
            place = pl.ds(pair * 2 * octet, 2 * octet)
            below = pl.ds(block_points + pair * 2 * octet, 2 * octet)
            crossed = []
            for k in (0, 2):
                crossed.append(jnp.where(even, green[k], shift(green[k + 1], 1)))
                crossed.append(jnp.where(even, shift(green[k], -1), green[k + 1]))
            for r in range(2):
                left, right = crossed[r], crossed[r + 2]
                minus = -left
                tops = (
                    jnp.where(low_lane, left, shift(right, 2)),
                    jnp.where(low_lane, shift(left, -2), right),
                )
                bottoms = (
                    jnp.where(low_lane, right, shift(minus, 2)),
                    jnp.where(low_lane, shift(right, -2), minus),
                )
                for i in range(2):
                    out_ref[b, r + 2 * i, place, :] = tops[i].astype(bf16)
                    out_ref[b, r + 2 * i, below, :] = bottoms[i].astype(bf16)

    lax.fori_loop(0, blocks_here, one_block, 0)


def circle(cycles):
    x = cycles - jnp.round(cycles)
    z = x * x * (math.pi * math.pi)
    sine, cosine = 0.0, 0.0
    for n in range(5, -1, -1):
        sine = sine * z + (-1.0) ** n / math.factorial(2 * n + 1)
    for n in range(6, -1, -1):
        cosine = cosine * z + (-1.0) ** n / math.factorial(2 * n)
    sine = sine * x * math.pi
    return 1.0 - 2.0 * sine * sine, 2.0 * sine * cosine


def turn(a, b):
    return a[0] * b[0] - a[1] * b[1], a[0] * b[1] + a[1] * b[0]


def arrival_order(first_step, steps):
    return sorted(range(steps), key=lambda step: -((first_step + step) & -2))


def spectra_kernel(blocks_here, samples, first_step, onset_scale, slip_scale, live_ref, green_ref, *refs):
    steps = (len(refs) - 3) // 2
    packed, outs = refs[:steps], refs[steps : 2 * steps]
    waves, total, held = refs[-3:]
    variations, block_points = packed[0].shape[2:]
    bins = green_ref.shape[3]
    first_bin = (lax.axis_index("cmp") * bins).astype(f32)
    quarter = lax.broadcasted_iota(jnp.int32, (variations, bins), 1) // 4
    total[...] = jnp.zeros_like(total)
    for place, step in enumerate(arrival_order(first_step, steps)):
        held[step * blocks_here : (step + 1) * blocks_here] = packed[place][...]
    steps_per_word, words = live_words(first_step + steps, blocks_here)
    for word in range(words):
        flags = jnp.max(live_ref[word])
        low = max(first_step, word * steps_per_word)
        high = min(first_step + steps, (word + 1) * steps_per_word)

        def visit(left):
            bit = 31 - lax.clz(left)
            place = bit + word * steps_per_word * blocks_here
            step = place // blocks_here
            local = place - step * blocks_here
            source = place - first_step * blocks_here
            onset = held[source, 0].astype(jnp.int32).astype(f32) + 32768.0
            slip = held[source, 1].astype(jnp.int32).astype(f32) * (1.0 / slip_scale)
            cycles = onset * (1.0 / (onset_scale * samples))
            one = circle(cycles)
            two = turn(one, one)
            four = turn(two, two)
            start = circle(cycles * first_bin)
            now = [(slip * start[0], slip * start[1])]
            now.append(turn(now[0], one))
            now.append(turn(now[0], two))
            now.append(turn(now[1], two))
            after = [turn(wave, four) for wave in now]
            double = 2.0 * four[0]
            for j in range(bins // 4):
                rows = pl.ds(j * variations, variations)
                for r in range(4):
                    waves[r, rows, 0:block_points] = now[r][0].astype(bf16)
                    waves[r, rows, block_points : 2 * block_points] = now[r][1].astype(bf16)
                later = [
                    (double * after[r][0] - now[r][0], double * after[r][1] - now[r][1])
                    for r in range(4)
                ]
                now, after = after, later
            for r in range(4):
                product = jnp.dot(waves[r], green_ref[local, r], preferred_element_type=f32)
                found = product[0:variations]
                for j in range(1, bins // 4):
                    found = jnp.where(
                        quarter == j, product[j * variations : (j + 1) * variations], found
                    )
                total[step - first_step, r] += found

            return left ^ jnp.left_shift(1, bit)

        first = (low - word * steps_per_word) * blocks_here
        last = (high - word * steps_per_word) * blocks_here
        flags = flags & ((1 << last) - (1 << first))
        lax.while_loop(lambda left: left != 0, visit, flags)
    for step in range(steps):
        outs[step][...] = total[step]


def spectra_call(first_step, onset_scale, slip_scale, live, green, received, name):
    steps = len(received)
    blocks_here, parts, variations, block_points = received[0].shape
    bins_here = green.shape[3]
    return pl.pallas_call(
        functools.partial(
            spectra_kernel, blocks_here, 4 * bins_here, first_step, onset_scale, slip_scale
        ),
        out_shape=[jax.ShapeDtypeStruct((4, variations, bins_here), f32)] * steps,
        in_specs=[VMEM] * (2 + steps),
        out_specs=[VMEM] * steps,
        scratch_shapes=[
            pltpu.VMEM((4, variations * bins_here // 4, 2 * block_points), bf16),
            pltpu.VMEM((steps, 4, variations, bins_here), f32),
            pltpu.VMEM((steps * blocks_here, parts, variations, block_points), jnp.int16),
        ],
        compiler_params=params(),
        cost_estimate=cost(steps * 1_000_000_000, 4_000_000 * steps),
        name=name,
    )(live, green, *[received[step] for step in arrival_order(first_step, steps)])


def three_products(left, table_high, table_low):
    rows = left.shape[0]
    coarse = left.astype(bf16)
    fine = (left - coarse.astype(f32)).astype(bf16)
    both = jnp.dot(
        jnp.concatenate([coarse, fine], axis=0), table_high, preferred_element_type=f32
    )
    return both[:rows] + both[rows:] + jnp.dot(coarse, table_low, preferred_element_type=f32)


def half_sign(bins, columns):
    odd = lax.broadcasted_iota(jnp.int32, (1, columns), 1) % bins % 2
    return (1 - 2 * odd * lax.axis_index("cmp")).astype(f32)


def band_kernel(
    bins, samples, row_ref, crossover_ref, high_ref, table_high, table_low, out_ref, weight_ref
):
    rows = jnp.concatenate([high_ref[0, :, c, :] for c in range(2)], axis=0)
    band = three_products(rows, table_high[...], table_low[...])
    sign = half_sign(bins, 2 * bins)
    out_ref[...] = -band * sign
    crossing = crossover_ref[row_ref[lax.axis_index("pt")]].astype(f32)
    column = lax.broadcasted_iota(jnp.int32, weight_ref.shape, 1) % bins
    taper = jnp.clip((crossing - column.astype(f32)) / taper_width + 0.5, 0.0, 1.0)
    weight_ref[...] = taper * (jnp.where(column == 0, 1.0, 2.0) / samples) * sign


def sum_kernel(bins_here, bins, band_ref, *refs):
    spectra, out_ref = refs[:-1], refs[-1]
    out_ref[...] = band_ref[...]
    half = lax.axis_index("cmp") * bins_here
    variations = spectra[0].shape[1]
    sums = []
    for r in range(4):
        piece = spectra[0][r]
        for other in spectra[1:]:
            piece = piece + other[r]
        sums.append(piece)
    lane = lax.broadcasted_iota(jnp.int32, (variations, bins_here), 1) % 4
    for k in range(4):
        spectrum = sums[0] if k == 0 else pltpu.roll(sums[0], bins_here - k, 1)
        for r in range(1, 4):
            moved = sums[r] if k == r else pltpu.roll(sums[r], (r - k) % bins_here, 1)
            spectrum = jnp.where(lane == r, moved, spectrum)
        place = pl.ds(pl.multiple_of((k // 2) * bins + half, bins_here), bins_here)
        rows = pl.ds((k % 2) * variations, variations)
        out_ref[rows, place] = out_ref[rows, place] + spectrum


def merge_kernel(own_ref, other_ref, weight_ref, high_ref, table_high, table_low, out_ref):
    excess = (own_ref[...] + other_ref[...]) * weight_ref[0:1]
    low = three_products(excess, table_high[...], table_low[...])
    variations = high_ref.shape[1]
    for c in range(2):
        out_ref[0, :, c, :] = high_ref[0, :, c, :] + low[c * variations : (c + 1) * variations]


def body(
    pt_size,
    strain_green,
    green_scale,
    mechanism,
    slip_amplitude,
    onset_time,
    rupture_row,
    rupture_blocks,
    block_count,
    crossover,
    high_band,
):
    points_here, strain_rows, bins_here = strain_green.shape
    blocks_here = green_scale.shape[0]
    block_points = points_here // blocks_here
    variations = slip_amplitude.shape[1]
    samples_here = high_band.shape[3]
    halves = 2
    bins = halves * bins_here
    samples = halves * samples_here
    assert slip_amplitude.shape[0] == 1 and pt_size & (pt_size - 1) == 0
    assert samples == 2 * bins and strain_rows == 24

    strain_lines = strain_green.reshape(points_here * strain_rows, bins_here)
    pack_shape = jax.ShapeDtypeStruct((blocks_here, 2, variations, block_points), jnp.int16)
    live_shape = jax.ShapeDtypeStruct((live_words(pt_size, blocks_here)[1], 8, 128), jnp.int32)
    onset_scale, slip_scale = 512.0, 1024.0
    *packed, live, scale_here, mechanism_here = pl.pallas_call(
        functools.partial(pack_kernel, blocks_here, block_points, onset_scale, slip_scale),
        out_shape=[pack_shape] * pt_size
        + [live_shape]
        + [jax.ShapeDtypeStruct(a.shape, a.dtype) for a in (green_scale, mechanism)],
        in_specs=[HBM] * 8,
        out_specs=[VMEM] * (pt_size + 3),
        scratch_shapes=scalar_scratch((rupture_row, rupture_blocks, block_count))
        + [pltpu.VMEM(a.shape, a.dtype) for a in (slip_amplitude, onset_time)]
        + [
            pltpu.VMEM((pt_size * blocks_here,) + pack_shape.shape[1:], jnp.int16),
            pltpu.SemaphoreType.DMA((5,)),
            pltpu.SemaphoreType.DMA((2,)),
        ],
        compiler_params=params(),
        name="pack",
    )(
        *in_hbm(
            rupture_row,
            rupture_blocks,
            block_count,
            slip_amplitude,
            onset_time,
            green_scale,
            mechanism,
            strain_lines,
        )
    )

    def swap(value, step):
        return lax.ppermute(value, "pt", [(i, i ^ step) for i in range(pt_size)])

    def exchange(values):
        moved = [swap(values[step], step) for step in range(pt_size - 1, 0, -1)]
        return [values[0]] + moved[::-1]

    received = exchange(packed)

    green = pl.pallas_call(
        functools.partial(green_kernel, pt_size),
        out_shape=jax.ShapeDtypeStruct((blocks_here, 4, 2 * block_points, bins_here), bf16),
        in_specs=[VMEM] * 4,
        out_specs=VMEM,
        scratch_shapes=[
            pltpu.VMEM((points_here, 8 * strain_rows + 64), f32),
        ],
        compiler_params=params(),
        cost_estimate=cost(2 * points_here * strain_rows * bins_here, 6_000_000),
        name="green",
    )(
        live,
        pltpu.with_memory_space_constraint(strain_lines, pltpu.VMEM),
        scale_here,
        mechanism_here,
    )

    sent = spectra_call(1, onset_scale, slip_scale, live, green, received[1:], "spectra")
    gathered = exchange([None] + list(sent))
    gathered[0], = spectra_call(0, onset_scale, slip_scale, live, green, received[:1], "own")

    table = fourier_table(bins, samples, samples_here)
    table_high, table_low = split_table(table)
    turned_high, turned_low = split_table(np.ascontiguousarray(table.T))
    rows = 2 * variations
    band, weight = pl.pallas_call(
        functools.partial(band_kernel, bins, samples),
        out_shape=[
            jax.ShapeDtypeStruct((rows, 2 * bins), f32),
            jax.ShapeDtypeStruct((8, 2 * bins), f32),
        ],
        in_specs=[SMEM] * 2 + [VMEM] * 3,
        out_specs=[VMEM] * 2,
        compiler_params=params(),
        cost_estimate=cost(6 * rows * samples_here * 2 * bins, 1_000_000),
        name="band",
    )(rupture_row, crossover, high_band, jnp.asarray(turned_high), jnp.asarray(turned_low))

    excess = pl.pallas_call(
        functools.partial(sum_kernel, bins_here, bins),
        out_shape=jax.ShapeDtypeStruct((rows, 2 * bins), f32),
        in_specs=[VMEM] * (1 + pt_size),
        out_specs=VMEM,
        compiler_params=params(),
        name="excess",
    )(band, *gathered[::-1])
    other = lax.ppermute(excess, "cmp", [(0, 1), (1, 0)])

    return pl.pallas_call(
        merge_kernel,
        out_shape=jax.ShapeDtypeStruct(high_band.shape, f32),
        in_specs=[VMEM] * 6,
        out_specs=VMEM,
        compiler_params=params(),
        name="merge",
    )(excess, other, weight, high_band, jnp.asarray(table_high), jnp.asarray(table_low))


def solution(mesh):
    assert mesh.shape["cmp"] == 2
    return jax.shard_map(
        functools.partial(body, mesh.shape["pt"]),
        mesh=mesh,
        in_specs=(
            P(("site", "pt"), None, "cmp"),
            P(("site", "pt"), None),
            P(None, "pt"),
            P("pt", "var", None),
            P("pt", "var", None),
            P(),
            P(),
            P(),
            P(),
            P(("site", "pt"), "var", None, "cmp"),
        ),
        out_specs=P(("site", "pt"), "var", None, "cmp"),
        check_vma=False,
    )
```

```python
import functools
import math

import jax
import jax.numpy as jnp
import ml_dtypes
import numpy as np
from jax import lax
from jax.experimental import pallas as pl
from jax.experimental.pallas import tpu as pltpu
from jax.sharding import PartitionSpec as P

taper_width = 8.0
f32 = jnp.float32
bf16 = jnp.bfloat16
highest = lax.Precision.HIGHEST
vmem_bytes = 32 * 1024 * 1024
SMEM = pl.BlockSpec(memory_space=pltpu.SMEM)
VMEM = pl.BlockSpec(memory_space=pltpu.VMEM)
HBM = pl.BlockSpec(memory_space=pltpu.HBM)


def in_hbm(*arrays):
    return [pltpu.with_memory_space_constraint(array, pltpu.HBM) for array in arrays]


def fetch(sources, targets, sems):
    copies = [
        pltpu.make_async_copy(source, target, sems.at[i])
        for i, (source, target) in enumerate(zip(sources, targets))
    ]
    for copy in copies:
        copy.start()
    return copies


def params():
    return pltpu.CompilerParams(vmem_limit_bytes=vmem_bytes)


def cost(flops, nbytes):
    return pl.CostEstimate(flops=flops, bytes_accessed=nbytes, transcendentals=0)


def split_table(table):
    high = table.astype(ml_dtypes.bfloat16)
    low = (table - high.astype(np.float64)).astype(ml_dtypes.bfloat16)
    return high, low


def fourier_table(bins, samples, samples_here):
    product = (np.arange(bins)[:, None] * np.arange(samples_here)[None, :]) % samples
    angle = product * (2.0 * np.pi / samples)
    return np.concatenate([np.cos(angle), -np.sin(angle)], axis=0)


def scalar_scratch(arrays):
    return [pltpu.SMEM(array.shape, array.dtype) for array in arrays]


def live_words(pt_size, blocks_here):
    steps_per_word = 30 // blocks_here
    return steps_per_word, pl.cdiv(pt_size, steps_per_word)


def pack_kernel(blocks_here, block_points, onset_scale, slip_scale, *refs):
    sources, later_sources, outs = refs[:5], refs[5:7], refs[8:-11]
    live_ref, later_targets = refs[-11], refs[-10:-8]
    targets, coded, sems, later_sems = refs[-8:-3], *refs[-3:]
    row_ref, blocks_ref, count_ref, slip_ref, onset_ref = targets
    copies = fetch(sources, targets, sems)
    later = fetch(later_sources, later_targets, later_sems)
    for copy in copies[:3]:
        copy.wait()
    me = lax.axis_index("pt")
    rupture = row_ref[me]
    steps_per_word, words = live_words(len(outs), blocks_here)
    for word in range(words):

        def one_step(step, flags):
            other = row_ref[jnp.bitwise_xor(me, step)]

            def one_slot(slot, flags):
                local = blocks_ref[other, slot] - me * blocks_here
                bit = jnp.left_shift(1, local + (step - word * steps_per_word) * blocks_here)
                return jnp.where((local >= 0) & (local < blocks_here), flags | bit, flags)

            return lax.fori_loop(0, count_ref[other], one_slot, flags)

        last = min(len(outs), (word + 1) * steps_per_word)
        flags = lax.fori_loop(word * steps_per_word, last, one_step, 0)
        live_ref[word] = jnp.full(live_ref.shape[1:], flags, jnp.int32)
    for copy in copies[3:]:
        copy.wait()

    def visit(slot, carry):
        block = blocks_ref[rupture, slot]
        owner = block // blocks_here
        local = block - owner * blocks_here
        offset = pl.multiple_of(slot * block_points, block_points)
        onset = jnp.round(onset_ref[0, :, pl.ds(offset, block_points)] * onset_scale)
        onset = jnp.clip(onset.astype(jnp.int32) - 32768, -32768, 32767).astype(jnp.int16)
        slip = slip_ref[0, :, pl.ds(offset, block_points)].astype(f32) * slip_scale
        slip = slip.astype(jnp.int32).astype(jnp.int16)
        place = jnp.bitwise_xor(me, owner) * blocks_here + local
        coded[place, 0] = onset
        coded[place, 1] = slip
        return carry

    lax.fori_loop(0, count_ref[rupture], visit, 0)
    for step, out in enumerate(outs):
        out[...] = coded[step * blocks_here : (step + 1) * blocks_here]
    for copy in later:
        copy.wait()


def three_parts(values):
    parts = []
    for _ in range(3):
        parts.append(values.astype(bf16).astype(f32))
        values = values - parts[-1]
    return parts


def green_kernel(
    steps, live_ref, strain_ref, scale_ref, mechanism_ref, out_ref, factor_ref
):
    rows, octet = 24, 8
    wide, depth = octet * rows, factor_ref.shape[1]
    blocks_here = scale_ref.shape[0]
    bins = strain_ref.shape[1]
    block_points = mechanism_ref.shape[1] // blocks_here
    per_block = block_points * rows

    column = lax.broadcasted_iota(jnp.int32, (18, depth), 1) % rows
    spread_six = column % 6 == lax.broadcasted_iota(jnp.int32, (18, depth), 0) % 6
    column = lax.broadcasted_iota(jnp.int32, (3 * rows, depth), 1) % rows
    spread_rows = column == lax.broadcasted_iota(jnp.int32, (3 * rows, depth), 0) % rows
    moments = lax.dot_general(
        jnp.concatenate(three_parts(mechanism_ref[...]), axis=0).astype(bf16),
        spread_six.astype(f32).astype(bf16),
        (((0,), (0,)), ((), ())),
        preferred_element_type=f32,
    )
    scales = jnp.dot(
        jnp.concatenate(three_parts(scale_ref[...]), axis=1).astype(bf16),
        spread_rows.astype(f32).astype(bf16),
        preferred_element_type=f32,
    )
    for b in range(blocks_here):
        place = slice(b * block_points, (b + 1) * block_points)
        factor_ref[place, :] = moments[place] * scales[b : b + 1]
    row = lax.broadcasted_iota(jnp.int32, (2 * octet, depth), 0)
    column = lax.broadcasted_iota(jnp.int32, (2 * octet, depth), 1)

    def point_masks(first_column):
        place = column - first_column
        mine = (place // rows == row % octet) & (place >= 0)
        part = (place % rows) // 6
        return [
            jnp.where(mine & (part == 2 * h + row // octet), 1.0, 0.0).astype(bf16)
            for h in range(2)
        ]

    spare = depth - wide
    usual, at_end = point_masks(0), point_masks(spare)
    lane = lax.broadcasted_iota(jnp.int32, (2 * octet, bins), 1) % 4
    even, low_lane = lane % 2 == 0, lane < 2

    def shift(values, by):
        return pltpu.roll(values, by % bins, 1)

    steps_per_word, words = live_words(steps, blocks_here)
    live = [jnp.max(live_ref[word]) for word in range(words)]

    def one_block(b, carry):
        flags = 0
        for step in range(steps):
            place = step % steps_per_word * blocks_here + b
            flags = flags | jnp.right_shift(live[step // steps_per_word], place)

        @pl.when(flags & 1 == 1)
        def _():
            place_block(b)

        return carry

    def place_block(b):
        for pair in range(block_points // (2 * octet)):
            spectra = [[], [], [], []]
            for half in range(2):
                first = pl.multiple_of(
                    b * block_points + pair * 2 * octet + half * octet, octet
                )
                here = factor_ref[pl.ds(first, octet)]
                last = (pair + 1) * 2 * octet == block_points and half == 1
                masks = at_end if last else usual
                if last:
                    here = pltpu.roll(here, spare, 1)
                here = jnp.concatenate([here, here], axis=0)
                coarse = here.astype(bf16)
                fine = (here - coarse.astype(f32)).astype(bf16)
                left = jnp.concatenate(
                    [coarse * masks[0], coarse * masks[1], fine * masks[0], fine * masks[1]],
                    axis=0,
                )
                begin = pl.multiple_of(first * rows - (spare if last else 0), 64)
                strain = strain_ref[pl.ds(begin, depth), :]
                both = jnp.dot(left, strain, preferred_element_type=f32)
                for k in range(4):
                    spectra[k].append(
                        both[k * octet : (k + 1) * octet]
                        + both[(k + 4) * octet : (k + 5) * octet]
                    )
            green = [jnp.concatenate(s, axis=0).astype(bf16).astype(f32) for s in spectra]
            place = pl.ds(pair * 2 * octet, 2 * octet)
            below = pl.ds(block_points + pair * 2 * octet, 2 * octet)
            crossed = []
            for k in (0, 2):
                crossed.append(jnp.where(even, green[k], shift(green[k + 1], 1)))
                crossed.append(jnp.where(even, shift(green[k], -1), green[k + 1]))
            for r in range(2):
                left, right = crossed[r], crossed[r + 2]
                minus = -left
                tops = (
                    jnp.where(low_lane, left, shift(right, 2)),
                    jnp.where(low_lane, shift(left, -2), right),
                )
                bottoms = (
                    jnp.where(low_lane, right, shift(minus, 2)),
                    jnp.where(low_lane, shift(right, -2), minus),
                )
                for i in range(2):
                    out_ref[b, r + 2 * i, place, :] = tops[i].astype(bf16)
                    out_ref[b, r + 2 * i, below, :] = bottoms[i].astype(bf16)

    lax.fori_loop(0, blocks_here, one_block, 0)


def circle(cycles):
    x = cycles - jnp.round(cycles)
    z = x * x * (math.pi * math.pi)
    sine, cosine = 0.0, 0.0
    for n in range(5, -1, -1):
        sine = sine * z + (-1.0) ** n / math.factorial(2 * n + 1)
    for n in range(6, -1, -1):
        cosine = cosine * z + (-1.0) ** n / math.factorial(2 * n)
    sine = sine * x * math.pi
    return 1.0 - 2.0 * sine * sine, 2.0 * sine * cosine


def turn(a, b):
    return a[0] * b[0] - a[1] * b[1], a[0] * b[1] + a[1] * b[0]


def arrival_order(first_step, steps):
    return sorted(range(steps), key=lambda step: -((first_step + step) & -2))


def spectra_kernel(blocks_here, samples, first_step, onset_scale, slip_scale, live_ref, green_ref, *refs):
    steps = (len(refs) - 3) // 2
    packed, outs = refs[:steps], refs[steps : 2 * steps]
    waves, total, held = refs[-3:]
    variations, block_points = packed[0].shape[2:]
    bins = green_ref.shape[3]
    first_bin = (lax.axis_index("cmp") * bins).astype(f32)
    quarter = lax.broadcasted_iota(jnp.int32, (variations, bins), 1) // 4
    total[...] = jnp.zeros_like(total)
    for place, step in enumerate(arrival_order(first_step, steps)):
        held[step * blocks_here : (step + 1) * blocks_here] = packed[place][...]
    steps_per_word, words = live_words(first_step + steps, blocks_here)
    for word in range(words):
        flags = jnp.max(live_ref[word])
        low = max(first_step, word * steps_per_word)
        high = min(first_step + steps, (word + 1) * steps_per_word)

        def visit(left):
            bit = 31 - lax.clz(left)
            place = bit + word * steps_per_word * blocks_here
            step = place // blocks_here
            local = place - step * blocks_here
            source = place - first_step * blocks_here
            onset = held[source, 0].astype(jnp.int32).astype(f32) + 32768.0
            slip = held[source, 1].astype(jnp.int32).astype(f32) * (1.0 / slip_scale)
            cycles = onset * (1.0 / (onset_scale * samples))
            one = circle(cycles)
            two = turn(one, one)
            four = turn(two, two)
            start = circle(cycles * first_bin)
            now = [(slip * start[0], slip * start[1])]
            now.append(turn(now[0], one))
            now.append(turn(now[0], two))
            now.append(turn(now[1], two))
            after = [turn(wave, four) for wave in now]
            double = 2.0 * four[0]
            for j in range(bins // 4):
                rows = pl.ds(j * variations, variations)
                for r in range(4):
                    waves[r, rows, 0:block_points] = now[r][0].astype(bf16)
                    waves[r, rows, block_points : 2 * block_points] = now[r][1].astype(bf16)
                later = [
                    (double * after[r][0] - now[r][0], double * after[r][1] - now[r][1])
                    for r in range(4)
                ]
                now, after = after, later
            for r in range(4):
                product = jnp.dot(waves[r], green_ref[local, r], preferred_element_type=f32)
                found = product[0:variations]
                for j in range(1, bins // 4):
                    found = jnp.where(
                        quarter == j, product[j * variations : (j + 1) * variations], found
                    )
                total[step - first_step, r] += found

            return left ^ jnp.left_shift(1, bit)

        first = (low - word * steps_per_word) * blocks_here
        last = (high - word * steps_per_word) * blocks_here
        flags = flags & ((1 << last) - (1 << first))
        lax.while_loop(lambda left: left != 0, visit, flags)
    for step in range(steps):
        outs[step][...] = total[step]


def spectra_call(first_step, onset_scale, slip_scale, live, green, received, name):
    steps = len(received)
    blocks_here, parts, variations, block_points = received[0].shape
    bins_here = green.shape[3]
    return pl.pallas_call(
        functools.partial(
            spectra_kernel, blocks_here, 4 * bins_here, first_step, onset_scale, slip_scale
        ),
        out_shape=[jax.ShapeDtypeStruct((4, variations, bins_here), f32)] * steps,
        in_specs=[VMEM] * (2 + steps),
        out_specs=[VMEM] * steps,
        scratch_shapes=[
            pltpu.VMEM((4, variations * bins_here // 4, 2 * block_points), bf16),
            pltpu.VMEM((steps, 4, variations, bins_here), f32),
            pltpu.VMEM((steps * blocks_here, parts, variations, block_points), jnp.int16),
        ],
        compiler_params=params(),
        cost_estimate=cost(steps * 1_000_000_000, 4_000_000 * steps),
        name=name,
    )(live, green, *[received[step] for step in arrival_order(first_step, steps)])


def three_products(left, table_high, table_low):
    rows = left.shape[0]
    coarse = left.astype(bf16)
    fine = (left - coarse.astype(f32)).astype(bf16)
    both = jnp.dot(
        jnp.concatenate([coarse, fine], axis=0), table_high, preferred_element_type=f32
    )
    return both[:rows] + both[rows:] + jnp.dot(coarse, table_low, preferred_element_type=f32)


def half_sign(bins, columns):
    odd = lax.broadcasted_iota(jnp.int32, (1, columns), 1) % bins % 2
    return (1 - 2 * odd * lax.axis_index("cmp")).astype(f32)


def band_kernel(
    bins, samples, row_ref, crossover_ref, high_ref, table_high, table_low, out_ref, weight_ref
):
    rows = jnp.concatenate([high_ref[0, :, c, :] for c in range(2)], axis=0)
    band = three_products(rows, table_high[...], table_low[...])
    sign = half_sign(bins, 2 * bins)
    out_ref[...] = -band * sign
    crossing = crossover_ref[row_ref[lax.axis_index("pt")]].astype(f32)
    column = lax.broadcasted_iota(jnp.int32, weight_ref.shape, 1) % bins
    taper = jnp.clip((crossing - column.astype(f32)) / taper_width + 0.5, 0.0, 1.0)
    weight_ref[...] = taper * (jnp.where(column == 0, 1.0, 2.0) / samples) * sign


def sum_kernel(bins_here, bins, band_ref, *refs):
    spectra, out_ref = refs[:-1], refs[-1]
    out_ref[...] = band_ref[...]
    half = lax.axis_index("cmp") * bins_here
    variations = spectra[0].shape[1]
    sums = []
    for r in range(4):
        piece = spectra[0][r]
        for other in spectra[1:]:
            piece = piece + other[r]
        sums.append(piece)
    lane = lax.broadcasted_iota(jnp.int32, (variations, bins_here), 1) % 4
    for k in range(4):
        spectrum = sums[0] if k == 0 else pltpu.roll(sums[0], bins_here - k, 1)
        for r in range(1, 4):
            moved = sums[r] if k == r else pltpu.roll(sums[r], (r - k) % bins_here, 1)
            spectrum = jnp.where(lane == r, moved, spectrum)
        place = pl.ds(pl.multiple_of((k // 2) * bins + half, bins_here), bins_here)
        rows = pl.ds((k % 2) * variations, variations)
        out_ref[rows, place] = out_ref[rows, place] + spectrum


def merge_kernel(own_ref, other_ref, weight_ref, high_ref, table_high, table_low, out_ref):
    excess = (own_ref[...] + other_ref[...]) * weight_ref[0:1]
    low = three_products(excess, table_high[...], table_low[...])
    variations = high_ref.shape[1]
    for c in range(2):
        out_ref[0, :, c, :] = high_ref[0, :, c, :] + low[c * variations : (c + 1) * variations]


def body(
    pt_size,
    strain_green,
    green_scale,
    mechanism,
    slip_amplitude,
    onset_time,
    rupture_row,
    rupture_blocks,
    block_count,
    crossover,
    high_band,
):
    points_here, strain_rows, bins_here = strain_green.shape
    blocks_here = green_scale.shape[0]
    block_points = points_here // blocks_here
    variations = slip_amplitude.shape[1]
    samples_here = high_band.shape[3]
    halves = 2
    bins = halves * bins_here
    samples = halves * samples_here
    assert slip_amplitude.shape[0] == 1 and pt_size & (pt_size - 1) == 0
    assert samples == 2 * bins and strain_rows == 24

    strain_lines = strain_green.reshape(points_here * strain_rows, bins_here)
    pack_shape = jax.ShapeDtypeStruct((blocks_here, 2, variations, block_points), jnp.int16)
    live_shape = jax.ShapeDtypeStruct((live_words(pt_size, blocks_here)[1], 8, 128), jnp.int32)
    onset_scale, slip_scale = 512.0, 1024.0
    *packed, live, scale_here, mechanism_here = pl.pallas_call(
        functools.partial(pack_kernel, blocks_here, block_points, onset_scale, slip_scale),
        out_shape=[pack_shape] * pt_size
        + [live_shape]
        + [jax.ShapeDtypeStruct(a.shape, a.dtype) for a in (green_scale, mechanism)],
        in_specs=[HBM] * 8,
        out_specs=[VMEM] * (pt_size + 3),
        scratch_shapes=scalar_scratch((rupture_row, rupture_blocks, block_count))
        + [pltpu.VMEM(a.shape, a.dtype) for a in (slip_amplitude, onset_time)]
        + [
            pltpu.VMEM((pt_size * blocks_here,) + pack_shape.shape[1:], jnp.int16),
            pltpu.SemaphoreType.DMA((5,)),
            pltpu.SemaphoreType.DMA((2,)),
        ],
        compiler_params=params(),
        name="pack",
    )(
        *in_hbm(
            rupture_row,
            rupture_blocks,
            block_count,
            slip_amplitude,
            onset_time,
            green_scale,
            mechanism,
            strain_lines,
        )
    )

    def swap(value, step):
        return lax.ppermute(value, "pt", [(i, i ^ step) for i in range(pt_size)])

    def exchange(values):
        moved = [swap(values[step], step) for step in range(pt_size - 1, 0, -1)]
        return [values[0]] + moved[::-1]

    received = exchange(packed)

    green = pl.pallas_call(
        functools.partial(green_kernel, pt_size),
        out_shape=jax.ShapeDtypeStruct((blocks_here, 4, 2 * block_points, bins_here), bf16),
        in_specs=[VMEM] * 4,
        out_specs=VMEM,
        scratch_shapes=[
            pltpu.VMEM((points_here, 8 * strain_rows + 64), f32),
        ],
        compiler_params=params(),
        cost_estimate=cost(2 * points_here * strain_rows * bins_here, 6_000_000),
        name="green",
    )(
        live,
        pltpu.with_memory_space_constraint(strain_lines, pltpu.VMEM),
        scale_here,
        mechanism_here,
    )

    near = spectra_call(1, onset_scale, slip_scale, live, green, received[1:2], "near")
    far = spectra_call(2, onset_scale, slip_scale, live, green, received[2:], "far")
    sent = list(near) + list(far)
    gathered = exchange([None] + list(sent))
    gathered[0], = spectra_call(0, onset_scale, slip_scale, live, green, received[:1], "own")

    table = fourier_table(bins, samples, samples_here)
    table_high, table_low = split_table(table)
    turned_high, turned_low = split_table(np.ascontiguousarray(table.T))
    rows = 2 * variations
    band, weight = pl.pallas_call(
        functools.partial(band_kernel, bins, samples),
        out_shape=[
            jax.ShapeDtypeStruct((rows, 2 * bins), f32),
            jax.ShapeDtypeStruct((8, 2 * bins), f32),
        ],
        in_specs=[SMEM] * 2 + [VMEM] * 3,
        out_specs=[VMEM] * 2,
        compiler_params=params(),
        cost_estimate=cost(6 * rows * samples_here * 2 * bins, 1_000_000),
        name="band",
    )(rupture_row, crossover, high_band, jnp.asarray(turned_high), jnp.asarray(turned_low))

    excess = pl.pallas_call(
        functools.partial(sum_kernel, bins_here, bins),
        out_shape=jax.ShapeDtypeStruct((rows, 2 * bins), f32),
        in_specs=[VMEM] * (1 + pt_size),
        out_specs=VMEM,
        compiler_params=params(),
        name="excess",
    )(band, *gathered[::-1])
    other = lax.ppermute(excess, "cmp", [(0, 1), (1, 0)])

    return pl.pallas_call(
        merge_kernel,
        out_shape=jax.ShapeDtypeStruct(high_band.shape, f32),
        in_specs=[VMEM] * 6,
        out_specs=VMEM,
        compiler_params=params(),
        name="merge",
    )(excess, other, weight, high_band, jnp.asarray(table_high), jnp.asarray(table_low))


def solution(mesh):
    assert mesh.shape["cmp"] == 2
    return jax.shard_map(
        functools.partial(body, mesh.shape["pt"]),
        mesh=mesh,
        in_specs=(
            P(("site", "pt"), None, "cmp"),
            P(("site", "pt"), None),
            P(None, "pt"),
            P("pt", "var", None),
            P("pt", "var", None),
            P(),
            P(),
            P(),
            P(),
            P(("site", "pt"), "var", None, "cmp"),
        ),
        out_specs=P(("site", "pt"), "var", None, "cmp"),
        check_vma=False,
    )
```
